128 devices in a mesh: gx: 4 (over z_hi, core), gy: 4 (over y), gz: 8 (over x, z_lo).
Axes of the slice: x: 4, y: 4, z: 4 (z_hi: 2, z_lo: 2; z = z_hi * 2 + z_lo), core: 2. Of those that a mesh axis runs over, the one named last changes fastest.
Arguments:
- cells: float32 [512, 5, 32, 1024], P(('gx', 'gy', 'gz')), may hold values from -4 to 16, as said below
- moves: int32 [128, 3, 2], replicated, may hold values from 0 to 3, as said below
- neighbours: int32 [64, 4], replicated, may hold values from 0 to 63, as said below
Outputs:
- updated: float32 [512, 5, 32, 1024], P(('gx', 'gy', 'gz'))
The draws below stay inside these ranges and needn't reach their ends.
Inputs may be any that keep to these rules, and one draw needn't show every extreme that they name: `cells`: density is 0.25 or more and the pressure (5/3 - 1)(E - |m|^2 / (2 rho)) is 0.25 or more in every cell. `moves`: the 2 slots of one device in one round are distinct. Neighbour relations are mutual (the -x neighbour of a patch's +x neighbour is that patch, likewise for y); no patch neighbours itself; counted with sides, the patches of one device have at most 2 neighbour links to any one other device, and some pair of devices has exactly 2 in every draw.
All inputs are finite; a program needn't handle non-finite values.
Results may differ from the reference program's by a relative error of at most 0.0003.
Values sent between devices are 32-bit elements; how exact they have to be, the bound alone decides.
No kernel may reach another device: no remote copies, remote signals or barrier semaphores. Data moves between devices by JAX's collectives and lax.ppermute only.
A program may use at most 128 MiB of HBM per device.

```python
import jax
import jax.numpy as jnp
from jax import lax

P_SIZE = 32
SLOTS = 4
MOVE = 2
PLANE = 16
PATCHES = 512
N_GX = 4
N_GY = 4
N_GZ = 8
DEVICES = 128


def draw_cells(key, part):
    key = jax.random.fold_in(key, 11)
    key_dens, key_vel, key_pres = jax.random.split(key, 3)
    shape = (PATCHES, P_SIZE, P_SIZE * P_SIZE)
    dens_lo, dens_hi, vel_top, pres_lo, pres_hi = (0.5, 4.0, 0.6, 0.5, 4.0)
    density = jnp.exp(jax.random.uniform(key_dens, shape, jnp.float32, jnp.log(dens_lo), jnp.log(dens_hi)))
    velocity = jax.random.uniform(key_vel, (3,) + shape, jnp.float32, -vel_top, vel_top)
    pressure = jnp.exp(jax.random.uniform(key_pres, shape, jnp.float32, jnp.log(pres_lo), jnp.log(pres_hi)))
    energy = pressure / (5.0 / 3.0 - 1.0) + 0.5 * density * jnp.sum(velocity * velocity, axis=0)
    fields = [density, density * velocity[0], density * velocity[1], density * velocity[2], energy]
    return jnp.stack(fields, axis=1).astype(jnp.float32)


def draw_moves(key, part):
    key = jax.random.fold_in(key, 12)
    row_keys = jax.random.split(key, DEVICES * 3)
    shuffled = jax.vmap(lambda row_key: jax.random.permutation(row_key, SLOTS))(row_keys)
    return shuffled[:, :MOVE].reshape(DEVICES, 3, MOVE).astype(jnp.int32)


def draw_neighbours(key, part):
    key = jax.random.fold_in(key, 13)
    key_shift, key_dev, key_slot = jax.random.split(key, 3)
    width_cells = 2 * N_GX
    height_cells = 2 * N_GY
    offsets = jax.random.randint(key_shift, (N_GY,), 0, 2)
    device_order = jax.random.permutation(key_dev, PLANE)
    slot_keys = jax.random.split(key_slot, PLANE)
    slot_order = jax.vmap(lambda slot_key: jax.random.permutation(slot_key, SLOTS))(slot_keys)
    rows_y = jnp.arange(height_cells)[:, None] + jnp.zeros((1, width_cells), jnp.int32)
    cols_x = jnp.arange(width_cells)[None, :] + jnp.zeros((height_cells, 1), jnp.int32)
    block_row = rows_y // 2
    moved_x = (cols_x - offsets[block_row]) % width_cells
    block_col = moved_x // 2
    within = rows_y % 2 * 2 + moved_x % 2
    owner = device_order[block_row * N_GX + block_col]
    grid_ids = owner * SLOTS + slot_order[owner, within]
    links = jnp.stack([jnp.roll(grid_ids, 1, axis=1), jnp.roll(grid_ids, -1, axis=1), jnp.roll(grid_ids, 1, axis=0), jnp.roll(grid_ids, -1, axis=0)], axis=-1)
    link_table = jnp.zeros((PLANE * SLOTS, 4), jnp.int32)
    return link_table.at[grid_ids.reshape(-1)].set(links.reshape(-1, 4).astype(jnp.int32))


def setup_inputs(seed: int = 0) -> dict:
    seeds = jax.random.split(jax.random.key(seed), 4)
    cells = draw_cells(jax.random.fold_in(seeds[3], 71), 0)
    moves = draw_moves(jax.random.fold_in(seeds[3], 71), 0)
    neighbours = draw_neighbours(jax.random.fold_in(seeds[3], 71), 0)
    return dict(cells=cells, moves=moves, neighbours=neighbours)


GAMMA = 5.0 / 3.0
DT_DX = 0.02

def primitives(conserved):
    density = conserved[0]
    velocity = conserved[1:4] / density
    pressure = (GAMMA - 1.0) * (conserved[4] - 0.5 * density * lax.optimization_barrier(jnp.sum(velocity * velocity, axis=0)))
    return jnp.concatenate([density[None], velocity, pressure[None]], axis=0)

def edge_values(prim_vals, stride):

    def shifted(count):
        return jnp.roll(prim_vals, -count * stride, axis=1)
    face_mid = 7.0 / 12.0 * (prim_vals + shifted(1)) - 1.0 / 12.0 * (shifted(-1) + shifted(2))
    face_mid = jnp.clip(face_mid, jnp.minimum(prim_vals, shifted(1)), jnp.maximum(prim_vals, shifted(1)))
    face_right = face_mid
    face_left = jnp.roll(face_mid, stride, axis=1)
    flatten = (face_right - prim_vals) * (prim_vals - face_left) <= 0.0
    face_left = jnp.where(flatten, prim_vals, face_left)
    face_right = jnp.where(flatten, prim_vals, face_right)
    spread_lr = face_right - face_left
    curvature = 6.0 * (prim_vals - 0.5 * (face_left + face_right))
    face_left = jnp.where(spread_lr * curvature > spread_lr * spread_lr, 3.0 * prim_vals - 2.0 * face_right, face_left)
    face_right = jnp.where(-spread_lr * spread_lr > spread_lr * curvature, 3.0 * prim_vals - 2.0 * face_left, face_right)
    return (face_left, face_right)

def euler_terms(prim_vals, normal):
    density = prim_vals[0]
    velocity = prim_vals[1:4]
    pressure = prim_vals[4]
    speed_n = velocity[normal]
    energy = pressure / (GAMMA - 1.0) + 0.5 * density * lax.optimization_barrier(jnp.sum(velocity * velocity, axis=0))
    state = jnp.stack([density, density * velocity[0], density * velocity[1], density * velocity[2], energy])
    momentum_flux = [density * velocity[component] * speed_n + (pressure if component == normal else 0.0) for component in range(3)]
    face_flux = jnp.stack([density * speed_n] + momentum_flux + [(energy + pressure) * speed_n])
    signal = jnp.abs(speed_n) + jnp.sqrt(GAMMA * pressure / density)
    return (state, face_flux, signal)

def direction_change(padded, stride, normal):
    flattened = padded.reshape(padded.shape[0], -1)
    prim_vals = primitives(flattened)
    face_left, face_right = edge_values(prim_vals, stride)
    state_left = face_right
    state_right = jnp.roll(face_left, -stride, axis=1)
    cons_left, flux_left, signal_left = euler_terms(state_left, normal)
    cons_right, flux_right, signal_right = euler_terms(state_right, normal)
    fastest = jnp.maximum(signal_left, signal_right)
    face_flux = 0.5 * (flux_left + flux_right) - 0.5 * fastest * (cons_right - cons_left)
    change = face_flux - jnp.roll(face_flux, stride, axis=1)
    return change.reshape(padded.shape)

def patch_update(own_patch, x_padded, y_padded, z_padded):
    edge_len = own_patch.shape[3]
    change = direction_change(x_padded, 1, 0)[..., 3:-3]
    change = change + direction_change(y_padded, edge_len, 1)[:, :, 3:-3, :]
    change = change + direction_change(z_padded, edge_len * edge_len, 2)[:, 3:-3]
    return (own_patch - DT_DX * change).reshape(own_patch.shape[0], edge_len, edge_len * edge_len)

def reference(cells, moves, neighbours):
    patch_count = cells.shape[0]
    device_count = patch_count // SLOTS
    device_ids = jnp.arange(device_count, dtype=jnp.int32)
    coordinates = [device_ids // (N_GY * N_GZ), device_ids // N_GZ % N_GY, device_ids % N_GZ]
    axis_sizes = [N_GX, N_GY, N_GZ]
    strides = [N_GY * N_GZ, N_GZ, 1]
    for round_id in range(3):
        flipped = coordinates[round_id] ^ axis_sizes[round_id] // 2
        partner = device_ids + (flipped - coordinates[round_id]) * strides[round_id]
        source = jnp.arange(patch_count, dtype=jnp.int32)
        dest_slot = device_ids[:, None] * SLOTS + moves[:, round_id, :]
        src_slot = partner[:, None] * SLOTS + moves[partner, round_id, :]
        source = source.at[dest_slot.reshape(-1)].set(src_slot.reshape(-1).astype(jnp.int32))
        cells = cells[source]
    edge_len = cells.shape[2]
    patch_grid = cells.reshape(N_GX * N_GY, N_GZ, SLOTS, 5, edge_len, edge_len, edge_len)

    def one_patch(flat_id):
        plane_id = flat_id // (N_GZ * SLOTS)
        layer_id = flat_id // SLOTS % N_GZ
        slot_id = flat_id % SLOTS
        own_patch = patch_grid[plane_id, layer_id, slot_id]
        links_of = neighbours[plane_id * SLOTS + slot_id]

        def patch_of(entry):
            return patch_grid[entry // SLOTS, layer_id, entry % SLOTS]
        x_padded = jnp.concatenate([patch_of(links_of[0])[..., edge_len - 3:], own_patch, patch_of(links_of[1])[..., :3]], axis=3)
        y_padded = jnp.concatenate([patch_of(links_of[2])[:, :, edge_len - 3:, :], own_patch, patch_of(links_of[3])[:, :, :3, :]], axis=2)
        below = patch_grid[plane_id, (layer_id - 1) % N_GZ, slot_id]
        above = patch_grid[plane_id, (layer_id + 1) % N_GZ, slot_id]
        z_padded = jnp.concatenate([below[:, edge_len - 3:], own_patch, above[:, :3]], axis=1)
        return patch_update(own_patch, x_padded, y_padded, z_padded)
    return lax.map(one_patch, jnp.arange(patch_count, dtype=jnp.int32))
```

```python
import functools

import jax
import jax.numpy as jnp
from jax import lax
from jax.experimental import pallas as pl
from jax.experimental.pallas import tpu as pltpu
from jax.sharding import PartitionSpec as P

GAMMA = 5.0 / 3.0
DT_DX = 0.02
EDGE = 32
GHOST = 3
SLOTS = 4
CHUNKS = 4
FIELDS = 5
PLANE = 16
LINKS = 16
ITEM_ROWS = 120
MIB = 1024 * 1024

F32 = jnp.float32
ANY = pl.BlockSpec(memory_space=pl.ANY)
SMEM = pl.BlockSpec(memory_space=pltpu.SMEM)
VMEM = pl.BlockSpec(memory_space=pltpu.VMEM)
CHUNK_SHAPE = (2, FIELDS, 64, 128)


def start_copy(plan, slot, rounds, chunk, cells, received, target, sem):
    taken = jnp.bool_(False)
    for r in reversed(range(rounds)):
        for j in range(2):
            hit = jnp.logical_and(plan[2 * r + j] == slot, jnp.logical_not(taken))

            @pl.when(hit)
            def _(r=r, j=j):
                pltpu.make_async_copy(received[r].at[j], target, sem).start()

            taken = jnp.logical_or(taken, hit)

    @pl.when(jnp.logical_not(taken))
    def _():
        pltpu.make_async_copy(cells.at[slot, :, chunk], target, sem).start()


def wait_copy(chunk, cells, target, sem):
    pltpu.make_async_copy(cells.at[0, :, chunk], target, sem).wait()


def pack_first_kernel(plan, cells, *refs):
    outs, sems = refs[:CHUNKS], refs[CHUNKS]
    copies = []
    for c in range(CHUNKS):
        for j in range(2):
            copies.append(
                pltpu.make_async_copy(cells.at[plan[j], :, c], outs[c].at[j], sems.at[c, j])
            )
    for copy in copies:
        copy.start()
    for copy in copies:
        copy.wait()


def pack_first(plan, cells):
    return pl.pallas_call(
        pack_first_kernel,
        out_shape=[jax.ShapeDtypeStruct(CHUNK_SHAPE, F32)] * CHUNKS,
        in_specs=[SMEM, ANY],
        out_specs=[VMEM] * CHUNKS,
        scratch_shapes=[pltpu.SemaphoreType.DMA((CHUNKS, 2))],
        compiler_params=pltpu.CompilerParams(vmem_limit_bytes=2 * MIB),
        name="pack_first",
    )(plan, cells)


def pack_kernel(r, chunk, plan, cells, *refs):
    received, out, sems = refs[:r], refs[r + 1], refs[r + 2]
    for j in range(2):
        start_copy(plan, plan[2 * r + j], r, chunk, cells, received, out.at[j], sems.at[j])
    for j in range(2):
        wait_copy(chunk, cells, out.at[j], sems.at[j])


def pack(r, chunk, plan, cells, received, after):
    return pl.pallas_call(
        functools.partial(pack_kernel, r, chunk),
        out_shape=jax.ShapeDtypeStruct(CHUNK_SHAPE, F32),
        in_specs=[SMEM, ANY] + [ANY] * (r + 1),
        out_specs=VMEM,
        scratch_shapes=[pltpu.SemaphoreType.DMA((2,))],
        compiler_params=pltpu.CompilerParams(vmem_limit_bytes=2 * MIB),
        name="pack",
    )(plan, cells, *received, after)


def swapped(block, axis):
    count = lax.axis_size(axis)
    return lax.ppermute(block, axis, [(i, i ^ (count // 2)) for i in range(count)])


def migrate(plan, cells):
    first = pack_first(plan, cells)
    got = [[swapped(block, "gx") for block in first], [None] * CHUNKS, [None] * CHUNKS]
    last = first[0]
    order = [(1, 0), (1, 1), (2, 0), (1, 2), (2, 1), (1, 3), (2, 2), (2, 3)]
    for r, c in order:
        last = pack(r, c, plan, cells, [got[i][c] for i in range(r)], last)
        got[r][c] = swapped(last, ("gx", "gy", "gz")[r])
    return got


def load_patches(plan, cells, received, patches, sems, wait):
    for k in range(SLOTS):
        for c in range(CHUNKS):
            if wait:
                wait_copy(c, cells, patches.at[k, :, c], sems.at[k, c])
            else:
                chunk_got = [received[r * CHUNKS + c] for r in range(3)]
                start_copy(plan, k, 3, c, cells, chunk_got, patches.at[k, :, c], sems.at[k, c])


def primitives(u):
    inv = 1.0 / u[0]
    v = [u[i] * inv for i in (1, 2, 3)]
    kinetic = u[1] * v[0] + u[2] * v[1] + u[3] * v[2]
    return [u[0]] + v + [(GAMMA - 1.0) * (u[4] - 0.5 * kinetic)]


def block_transpose(b):
    lane = lax.broadcasted_iota(jnp.int32, (8, 128), 1)
    low = lane < 64
    even = (lane & 32) == 0

    def rolled(x, shift):
        return pltpu.roll(x, shift, 1)

    a0 = jnp.where(low, b[0], rolled(b[2], 64))
    a2 = jnp.where(low, rolled(b[0], 64), b[2])
    a1 = jnp.where(low, b[1], rolled(b[3], 64))
    a3 = jnp.where(low, rolled(b[1], 64), b[3])
    return [
        jnp.where(even, a0, rolled(a1, 32)),
        jnp.where(even, rolled(a0, 96), a1),
        jnp.where(even, a2, rolled(a3, 32)),
        jnp.where(even, rolled(a2, 96), a3),
    ]


def face_block(turned, side, f, layer, g):
    if side == 0:
        return turned[f, g, pl.ds(layer, 8, stride=EDGE), :]
    if side == 1:
        return turned[f, g, pl.ds(EDGE - GHOST + layer, 8, stride=EDGE), :]
    if side == 2:
        return turned[f, 0, pl.ds(layer * EDGE + 8 * g, 8), :]
    return turned[f, 3, pl.ds((8 - GHOST + layer) * EDGE + 8 * g, 8), :]


def faces_kernel(plan, place, links, cells, *refs):
    received = refs[: 3 * CHUNKS]
    turned, send, own_items, z_first, z_last = refs[3 * CHUNKS : 3 * CHUNKS + 5]
    patches, prim, items, sems, item_sems = refs[3 * CHUNKS + 5 :]
    load_patches(plan, cells, received, patches, sems, False)
    load_patches(plan, cells, received, patches, sems, True)

    def turn(g, carry):
        for half in range(2):
            rows = pl.ds(pl.multiple_of((2 * g + half) * 8, 8), 8)
            for k in range(SLOTS):
                for c in range(CHUNKS):
                    w = primitives([patches[k, f, c, rows, :] for f in range(FIELDS)])
                    for f in range(FIELDS):
                        prim[f, pl.ds((k * CHUNKS + c) * 8, 8), :] = w[f]
            for f in range(FIELDS):
                turned[f, g, pl.ds(half * 128, 128), :] = jnp.transpose(prim[f])
        return carry

    lax.fori_loop(0, 4, turn, 0)

    for side in range(4):
        for f in range(FIELDS):
            for layer in range(GHOST):
                blocks = block_transpose([face_block(turned, side, f, layer, g) for g in range(4)])
                for k in range(SLOTS):
                    items[k * 4 + side, pl.ds((f * GHOST + layer) * 8, 8), :] = blocks[k]

    me = place[0]
    owners = [links[me * LINKS + i] // SLOTS for i in range(LINKS)]
    for i in range(LINKS):
        rank = jnp.int32(0)
        for j in range(i):
            rank = rank + (owners[j] == owners[i]).astype(jnp.int32)
        rank = jnp.minimum(rank, 1)

        @pl.when(owners[i] != me)
        def _(i=i, rank=rank):
            pltpu.make_async_copy(items.at[i], send.at[owners[i], rank], item_sems.at[i]).start()

        @pl.when(owners[i] == me)
        def _(i=i):
            pltpu.make_async_copy(items.at[i], own_items.at[i], item_sems.at[i]).start()

    for k in range(SLOTS):
        for f in range(FIELDS):
            for layer in range(GHOST):
                z_first[k, f, layer] = patches[k, f, 0, pl.ds(layer, 8, stride=8), :]
                z_last[k, f, layer] = patches[k, f, CHUNKS - 1, pl.ds(5 + layer, 8, stride=8), :]

    for i in range(LINKS):
        pltpu.make_async_copy(items.at[i], own_items.at[i], item_sems.at[i]).wait()


def faces(plan, place, links, cells, received):
    z_shape = jax.ShapeDtypeStruct((SLOTS, FIELDS, GHOST, 8, 128), F32)
    return pl.pallas_call(
        faces_kernel,
        out_shape=[
            jax.ShapeDtypeStruct((FIELDS, 4, 256, 128), F32),
            jax.ShapeDtypeStruct((PLANE, 2, ITEM_ROWS, 128), F32),
            jax.ShapeDtypeStruct((LINKS, ITEM_ROWS, 128), F32),
            z_shape,
            z_shape,
        ],
        in_specs=[SMEM, SMEM, SMEM, ANY] + [ANY] * (3 * CHUNKS),
        out_specs=[VMEM, ANY, ANY, VMEM, VMEM],
        scratch_shapes=[
            pltpu.VMEM((SLOTS, FIELDS, CHUNKS, 64, 128), F32),
            pltpu.VMEM((FIELDS, 128, 128), F32),
            pltpu.VMEM((LINKS, ITEM_ROWS, 128), F32),
            pltpu.SemaphoreType.DMA((SLOTS, CHUNKS)),
            pltpu.SemaphoreType.DMA((LINKS,)),
        ],
        compiler_params=pltpu.CompilerParams(vmem_limit_bytes=12 * MIB),
        name="faces",
    )(plan, place, links, cells, *received)


def clamped(x, y):
    return jnp.minimum(jnp.maximum(x, jnp.minimum(y, 0.0)), jnp.maximum(y, 0.0))


def euler_terms(w, normal):
    density, velocity, pressure = w[0], w[1:4], w[4]
    speed = velocity[normal]
    momentum = [density * v for v in velocity]
    kinetic = momentum[0] * velocity[0] + momentum[1] * velocity[1] + momentum[2] * velocity[2]
    energy = 1.5 * pressure + 0.5 * kinetic
    flux = [momentum[normal]]
    for i in range(3):
        term = momentum[i] * speed
        flux.append(term + pressure if i == normal else term)
    flux.append((energy + pressure) * speed)
    stiff = GAMMA * pressure
    signal = jnp.abs(speed) + stiff * lax.rsqrt(stiff * density)
    return [density] + momentum + [energy], flux, signal


def sweep(get, put, normal):
    w, d, a = {}, {}, {}
    b, prev_flux, left = {}, None, None
    for i in range(-3, EDGE + GHOST):
        w[i] = get(i)
        if i == -3:
            continue
        d[i - 1] = [hi - lo for hi, lo in zip(w[i], w[i - 1])]
        if i < 0:
            continue
        m = i - 2
        a[m] = [
            clamped(0.5 * mid - (1.0 / 12.0) * (up - down), mid)
            for down, mid, up in zip(d[m - 1], d[m], d[m + 1])
        ]
        b[m + 1] = [mid - part for mid, part in zip(d[m], a[m])]
        if m < -1:
            continue
        lower = [v - clamped(y, 2.0 * x) for v, x, y in zip(w[m], a[m], b[m])]
        upper = [v + clamped(x, 2.0 * y) for v, x, y in zip(w[m], a[m], b[m])]
        if left is not None:
            right = euler_terms(lower, normal)
            fastest = jnp.maximum(left[2], right[2])
            flux = [
                gl + gr - fastest * (ur - ul)
                for gl, gr, ul, ur in zip(left[1], right[1], left[0], right[0])
            ]
            if prev_flux is not None:
                put(m - 1, [new - old for new, old in zip(flux, prev_flux)])
            prev_flux = flux
        left = euler_terms(upper, normal)


def update_kernel(plan, place, links, cells, *refs):
    received = refs[: 3 * CHUNKS]
    turned, arrived, own_items, z_below, z_above, out = refs[3 * CHUNKS : 3 * CHUNKS + 6]
    patches, items, ghosts, change, z_change, sems, item_sems = refs[3 * CHUNKS + 6 :]
    load_patches(plan, cells, received, patches, sems, False)

    me = place[0]
    for k in range(SLOTS):
        for side in range(4):
            i = k * 4 + side
            entry = links[me * LINKS + i]
            owner = entry // SLOTS
            source = (entry % SLOTS) * 4 + (side ^ 1)
            rank = jnp.int32(0)
            for j in range(LINKS - 1):
                same = jnp.logical_and(links[owner * LINKS + j] // SLOTS == me, j < source)
                rank = rank + same.astype(jnp.int32)
            rank = jnp.minimum(rank, 1)

            @pl.when(owner != me)
            def _(i=i, owner=owner, rank=rank):
                pltpu.make_async_copy(arrived.at[owner, rank], items.at[i], item_sems.at[i]).start()

            @pl.when(owner == me)
            def _(i=i, source=source):
                pltpu.make_async_copy(own_items.at[source], items.at[i], item_sems.at[i]).start()

    load_patches(plan, cells, received, patches, sems, True)

    def z_sweep(k, carry):
        def get(i):
            if i < 0:
                u = [z_below[k, f, i + GHOST] for f in range(FIELDS)]
            elif i >= EDGE:
                u = [z_above[k, f, i - EDGE] for f in range(FIELDS)]
            else:
                u = [patches[k, f, i // 8, pl.ds(i % 8, 8, stride=8), :] for f in range(FIELDS)]
            return primitives(u)

        def put(i, values):
            for f in range(FIELDS):
                z_change[k, f, i // 8, pl.ds(i % 8, 8, stride=8), :] = values[f]

        sweep(get, put, 2)
        return carry

    lax.fori_loop(0, SLOTS, z_sweep, 0)

    for i in range(LINKS):
        pltpu.make_async_copy(own_items.at[i], items.at[i], item_sems.at[i]).wait()
    for side in range(4):
        for n in range(FIELDS * GHOST):
            blocks = block_transpose([items[k * 4 + side, pl.ds(n * 8, 8), :] for k in range(SLOTS)])
            for g in range(4):
                ghosts[side, n, g] = blocks[g]

    def y_sweep(g, carry):
        def rows(i):
            return pl.ds(pl.multiple_of((i % 8) * EDGE + 8 * g, 8), 8)

        def get(i):
            if i < 0:
                return [ghosts[2, f * GHOST + i + GHOST, g] for f in range(FIELDS)]
            if i >= EDGE:
                return [ghosts[3, f * GHOST + i - EDGE, g] for f in range(FIELDS)]
            return [turned[f, i // 8, rows(i), :] for f in range(FIELDS)]

        def put(i, values):
            for f in range(FIELDS):
                change[f, i // 8, rows(i), :] = values[f]

        sweep(get, put, 1)
        return carry

    lax.fori_loop(0, 4, y_sweep, 0)

    def x_sweep(g, carry):
        def get(i):
            if i < 0:
                return [ghosts[0, f * GHOST + i + GHOST, g] for f in range(FIELDS)]
            if i >= EDGE:
                return [ghosts[1, f * GHOST + i - EDGE, g] for f in range(FIELDS)]
            return [turned[f, g, pl.ds(i, 8, stride=EDGE), :] for f in range(FIELDS)]

        def put(i, values):
            for f in range(FIELDS):
                rows = pl.ds(i, 8, stride=EDGE)
                change[f, g, rows, :] = change[f, g, rows, :] + values[f]

        sweep(get, put, 0)
        return carry

    lax.fori_loop(0, 4, x_sweep, 0)

    def finish(g, carry):
        for f in range(FIELDS):
            for half in range(2):
                rows = pl.ds(pl.multiple_of((2 * g + half) * 8, 8), 8)
                back = jnp.transpose(change[f, g, pl.ds(half * 128, 128), :])
                for k in range(SLOTS):
                    for c in range(CHUNKS):
                        n = (k * CHUNKS + c) * 8
                        total = back[n : n + 8] + z_change[k, f, c, rows, :]
                        out[k, f, c, rows, :] = patches[k, f, c, rows, :] - (0.5 * DT_DX) * total
        return carry

    lax.fori_loop(0, 4, finish, 0)


def update(plan, place, links, cells, received, turned, arrived, own_items, z_below, z_above):
    patch_shape = (SLOTS, FIELDS, CHUNKS, 64, 128)
    return pl.pallas_call(
        update_kernel,
        out_shape=jax.ShapeDtypeStruct(patch_shape, F32),
        in_specs=[SMEM, SMEM, SMEM, ANY] + [ANY] * (3 * CHUNKS) + [VMEM, ANY, ANY, VMEM, VMEM],
        out_specs=VMEM,
        scratch_shapes=[
            pltpu.VMEM(patch_shape, F32),
            pltpu.VMEM((LINKS, ITEM_ROWS, 128), F32),
            pltpu.VMEM((4, FIELDS * GHOST, 4, 8, 128), F32),
            pltpu.VMEM((FIELDS, 4, 256, 128), F32),
            pltpu.VMEM(patch_shape, F32),
            pltpu.SemaphoreType.DMA((SLOTS, CHUNKS)),
            pltpu.SemaphoreType.DMA((LINKS,)),
        ],
        compiler_params=pltpu.CompilerParams(vmem_limit_bytes=20 * MIB),
        name="update",
    )(plan, place, links, cells, *received, turned, arrived, own_items, z_below, z_above)


def local(cells, moves, neighbours):
    tiled = cells.reshape(SLOTS, FIELDS, CHUNKS, 8, 8, 128).transpose(0, 1, 2, 4, 3, 5)
    tiled = tiled.reshape(SLOTS, FIELDS, CHUNKS, 64, 128)
    plan = moves[lax.axis_index(("gx", "gy", "gz"))].reshape(-1)
    place = lax.axis_index(("gx", "gy")).reshape(1)
    links = neighbours.reshape(-1)

    got = migrate(plan, tiled)
    received = [block for row in got for block in row]
    turned, send, own_items, z_first, z_last = faces(plan, place, links, tiled, received)

    layers = lax.axis_size("gz")
    up = [(i, (i + 1) % layers) for i in range(layers)]
    down = [(j, i) for i, j in up]
    z_below = lax.ppermute(z_last, "gz", up)
    z_above = lax.ppermute(z_first, "gz", down)
    arrived = lax.all_to_all(send, ("gx", "gy"), 0, 0, tiled=True)
    result = update(
        plan, place, links, tiled, received, turned, arrived, own_items, z_below, z_above
    )
    result = result.reshape(SLOTS, FIELDS, CHUNKS, 8, 8, 128).transpose(0, 1, 2, 4, 3, 5)
    return result.reshape(cells.shape)


def solution(mesh):
    return jax.shard_map(
        local,
        mesh=mesh,
        in_specs=(P(("gx", "gy", "gz"), None, None, None), P(), P()),
        out_specs=P(("gx", "gy", "gz"), None, None, None),
        check_vma=False,
    )
```

```python
import functools

import jax
import jax.numpy as jnp
from jax import lax
from jax.experimental import pallas as pl
from jax.experimental.pallas import tpu as pltpu
from jax.sharding import PartitionSpec as P

GAMMA = 5.0 / 3.0
DT_DX = 0.02
EDGE = 32
GHOST = 3
SLOTS = 4
LAYERS = 4
FIELDS = 5
PLANE = 16
LINKS = 16
GROUPS = ((0, 1, 2), (3, 4))
ITEM_ROWS = FIELDS * GHOST * 8
PATCH_SHAPE = (FIELDS, SLOTS, LAYERS, 64, 128)
TURNED_SHAPE = (FIELDS, 4, 256, 128)
MIB = 1024 * 1024

F32 = jnp.float32
ANY = pl.BlockSpec(memory_space=pl.ANY)
HBM = pl.BlockSpec(memory_space=pltpu.HBM)
SMEM = pl.BlockSpec(memory_space=pltpu.SMEM)
VMEM = pl.BlockSpec(memory_space=pltpu.VMEM)
LONG = pl.CostEstimate(flops=10**12, bytes_accessed=10**10, transcendentals=10**10)
CHUNK_SHAPE = (2, LAYERS, 64, 128)


def held(x):
    return pltpu.with_memory_space_constraint(x, pltpu.HBM)


def start_copy(plan, slot, rounds, field, cells, received, target, sem, part=slice(None)):
    taken = jnp.bool_(False)
    for r in reversed(range(rounds)):
        for j in range(2):
            hit = jnp.logical_and(plan[2 * r + j] == slot, jnp.logical_not(taken))

            @pl.when(hit)
            def _(r=r, j=j):
                pltpu.make_async_copy(received[r].at[j, part], target, sem).start()

            taken = jnp.logical_or(taken, hit)

    @pl.when(jnp.logical_not(taken))
    def _():
        pltpu.make_async_copy(cells.at[slot, field, part], target, sem).start()


def pack_kernel(sends, taken, plan, cells, *refs):
    received, refs = refs[:taken], refs[-len(sends) - 1 :]
    outs, sems = refs[:-1], refs[-1]
    at = 0
    for n, (r, f) in enumerate(sends):
        got = received[at : at + r]
        at += r
        for j in range(2):
            start_copy(plan, plan[2 * r + j], r, f, cells, got, outs[n].at[j], sems.at[n, j])
    for n, (r, f) in enumerate(sends):
        for j in range(2):
            pltpu.make_async_copy(cells.at[0, f], outs[n].at[j], sems.at[n, j]).wait()


def pack(sends, plan, cells, received, after):
    return pl.pallas_call(
        functools.partial(pack_kernel, sends, len(received)),
        out_shape=[jax.ShapeDtypeStruct(CHUNK_SHAPE, F32)] * len(sends),
        in_specs=[SMEM, HBM] + [ANY] * (len(received) + len(after)),
        out_specs=[VMEM] * len(sends),
        scratch_shapes=[pltpu.SemaphoreType.DMA((len(sends), 2))],
        compiler_params=pltpu.CompilerParams(vmem_limit_bytes=4 * MIB),
        name="pack",
    )(plan, held(cells), *received, *after)


def swapped(block, axis):
    count = lax.axis_size(axis)
    return lax.ppermute(block, axis, [(i, i ^ (count // 2)) for i in range(count)])


WAVES = (
    ([(0, 0), (0, 1), (0, 2), (0, 3), (0, 4)], []),
    ([(1, 0)], []),
    ([(1, 1)], []),
    ([(1, 2), (2, 0)], []),
    ([(1, 3), (2, 1)], []),
    ([(1, 4), (2, 2)], [(2, 0)]),
    ([(2, 3)], [(2, 1)]),
    ([(2, 4)], [(2, 2)]),
)


def migrate(plan, cells):
    got, last = {}, []
    for sends, awaited in WAVES:
        received = [got[i, f] for r, f in sends for i in range(r)]
        after = list(last[-1:]) + [got[at] for at in awaited]
        last = pack(sends, plan, cells, received, after)
        for (r, f), block in zip(sends, last):
            got[r, f] = swapped(block, ("gx", "gy", "gz")[r])
    return got, last[-1]


def primitives(u):
    inv = 1.0 / u[0]
    v = [u[i] * inv for i in (1, 2, 3)]
    kinetic = u[1] * v[0] + u[2] * v[1] + u[3] * v[2]
    return [u[0]] + v + [(GAMMA - 1.0) * (u[4] - 0.5 * kinetic)]


def block_transpose(b):
    lane = lax.broadcasted_iota(jnp.int32, (8, 128), 1)
    low = lane < 64
    even = (lane & 32) == 0

    def rolled(x, shift):
        return pltpu.roll(x, shift, 1)

    a0 = jnp.where(low, b[0], rolled(b[2], 64))
    a2 = jnp.where(low, rolled(b[0], 64), b[2])
    a1 = jnp.where(low, b[1], rolled(b[3], 64))
    a3 = jnp.where(low, rolled(b[1], 64), b[3])
    return [
        jnp.where(even, a0, rolled(a1, 32)),
        jnp.where(even, rolled(a0, 96), a1),
        jnp.where(even, a2, rolled(a3, 32)),
        jnp.where(even, rolled(a2, 96), a3),
    ]


def face_block(turned, side, f, layer, g):
    if side == 0:
        return turned[f, g, pl.ds(layer, 8, stride=EDGE), :]
    if side == 1:
        return turned[f, g, pl.ds(EDGE - GHOST + layer, 8, stride=EDGE), :]
    if side == 2:
        return turned[f, 0, pl.ds(layer * EDGE + 8 * g, 8), :]
    return turned[f, 3, pl.ds((8 - GHOST + layer) * EDGE + 8 * g, 8), :]


def faces_kernel(fields, plan, place, links, cells, *refs):
    count, first, last = len(fields), fields[0], fields[0] > 0
    received = refs[: 3 * count]
    refs = refs[3 * count + 1 + 4 * last :]
    patches_out, turned_out, send, own_items = refs[:4]
    patches, turned, items, sems, item_sems, out_sems = refs[-6:]
    for n, f in enumerate(fields):
        got = received[3 * n : 3 * n + 3]
        for k in range(SLOTS):
            start_copy(plan, k, 3, f, cells, got, patches.at[n, k], sems.at[n, k])
    mine = pl.ds(first, count)
    outs = [
        pltpu.make_async_copy(patches, patches_out.at[mine], out_sems.at[0]),
        pltpu.make_async_copy(turned, turned_out.at[mine], out_sems.at[1]),
    ]
    for n, f in enumerate(fields):
        for k in range(SLOTS):
            pltpu.make_async_copy(cells.at[k, f], patches.at[n, k], sems.at[n, k]).wait()

        def turn(g, carry, n=n):
            for half in range(2):
                rows = pl.ds(pl.multiple_of((2 * g + half) * 8, 8), 8)
                tiles = [patches[n, k, c, rows, :] for k in range(SLOTS) for c in range(LAYERS)]
                turned[n, g, pl.ds(half * 128, 128), :] = jnp.transpose(
                    jnp.concatenate(tiles, axis=0)
                )
            return carry

        lax.fori_loop(0, 4, turn, 0)
    for copy in outs:
        copy.start()

    me = place[0]
    owners = [links[me * LINKS + i] // SLOTS for i in range(LINKS)]
    rows = pl.ds(first * GHOST * 8, count * GHOST * 8)
    for side in range(4):
        for n in range(count):
            for layer in range(GHOST):
                blocks = block_transpose([face_block(turned, side, n, layer, g) for g in range(4)])
                for k in range(SLOTS):
                    items[k * 4 + side, pl.ds((n * GHOST + layer) * 8, 8), :] = blocks[k]
        for i in range(side, LINKS, 4):
            rank = jnp.int32(0)
            for j in range(i):
                rank = rank + (owners[j] == owners[i]).astype(jnp.int32)
            rank = jnp.minimum(rank, 1)

            @pl.when(owners[i] != me)
            def _(i=i, rank=rank):
                target = send.at[owners[i], rank, rows]
                pltpu.make_async_copy(items.at[i], target, item_sems.at[i]).start()

            @pl.when(owners[i] == me)
            def _(i=i):
                target = own_items.at[i, rows]
                pltpu.make_async_copy(items.at[i], target, item_sems.at[i]).start()

    for i in range(LINKS):
        pltpu.make_async_copy(items.at[i], own_items.at[i, rows], item_sems.at[i]).wait()
    for copy in outs:
        copy.wait()


def faces(fields, plan, place, links, cells, received, after, carried):
    count, first = len(fields), fields[0]
    scratch = [
        pltpu.VMEM((count,) + PATCH_SHAPE[1:], F32),
        pltpu.VMEM((count,) + TURNED_SHAPE[1:], F32),
        pltpu.VMEM((LINKS, count * GHOST * 8, 128), F32),
        pltpu.SemaphoreType.DMA((count, SLOTS)),
        pltpu.SemaphoreType.DMA((LINKS,)),
        pltpu.SemaphoreType.DMA((2,)),
    ]
    inputs = [held(cells)] + list(received) + [after] + [held(x) for x in carried]
    return pl.pallas_call(
        functools.partial(faces_kernel, fields),
        out_shape=[
            pltpu.HBM(PATCH_SHAPE, F32),
            pltpu.HBM(TURNED_SHAPE, F32),
            pltpu.HBM((PLANE, 2, ITEM_ROWS, 128), F32),
            pltpu.HBM((LINKS, ITEM_ROWS, 128), F32),
        ],
        in_specs=[SMEM] * 3 + [HBM] + [ANY] * (3 * count + 1) + [HBM] * len(carried),
        out_specs=[HBM] * 4,
        scratch_shapes=scratch,
        input_output_aliases={3 * count + 5 + i: i for i in range(len(carried))},
        compiler_params=pltpu.CompilerParams(vmem_limit_bytes=16 * MIB),
        name="faces",
    )(plan, place, links, *inputs)


def ends_kernel(plan, cells, patches, *refs):
    late = GROUPS[1]
    received = refs[: 3 * len(late)]
    z_first, z_last, ends, sems = refs[3 * len(late) :]
    loads = []
    for e in range(2):
        source = patches.at[pl.ds(0, late[0]), :, e * (LAYERS - 1)]
        load = pltpu.make_async_copy(source, ends.at[e, pl.ds(0, late[0])], sems.at[e, 0, 0])
        load.start()
        loads.append(load)
    places = [(n, k, e) for n in range(len(late)) for k in range(SLOTS) for e in range(2)]
    for n, k, e in places:
        f, got, layer = late[n], received[3 * n : 3 * n + 3], e * (LAYERS - 1)
        start_copy(plan, k, 3, f, cells, got, ends.at[e, f, k], sems.at[e, n + 1, k], layer)
    for load in loads:
        load.wait()
    for n, k, e in places:
        f = late[n]
        pltpu.make_async_copy(cells.at[k, f, 0], ends.at[e, f, k], sems.at[e, n + 1, k]).wait()
    for f in range(FIELDS):
        for k in range(SLOTS):
            for layer in range(GHOST):
                z_first[k, f, layer] = ends[0, f, k, pl.ds(layer, 8, stride=8), :]
                z_last[k, f, layer] = ends[1, f, k, pl.ds(5 + layer, 8, stride=8), :]


def z_ends(plan, cells, patches, received):
    z_shape = jax.ShapeDtypeStruct((SLOTS, FIELDS, GHOST, 8, 128), F32)
    return pl.pallas_call(
        ends_kernel,
        out_shape=[z_shape, z_shape],
        in_specs=[SMEM, HBM, HBM] + [ANY] * len(received),
        out_specs=[VMEM, VMEM],
        scratch_shapes=[
            pltpu.VMEM((2, FIELDS, SLOTS, 64, 128), F32),
            pltpu.SemaphoreType.DMA((2, 1 + len(GROUPS[1]), SLOTS)),
        ],
        compiler_params=pltpu.CompilerParams(vmem_limit_bytes=6 * MIB),
        name="z_ends",
    )(plan, held(cells), held(patches), *received)


def clamped(x, y):
    return jnp.minimum(jnp.maximum(x, jnp.minimum(y, 0.0)), jnp.maximum(y, 0.0))


def euler_terms(w, normal):
    density, velocity, pressure = w[0], w[1:4], w[4]
    speed = velocity[normal]
    momentum = [density * v for v in velocity]
    kinetic = momentum[0] * velocity[0] + momentum[1] * velocity[1] + momentum[2] * velocity[2]
    energy = 1.5 * pressure + 0.5 * kinetic
    flux = [momentum[normal]]
    for i in range(3):
        term = momentum[i] * speed
        flux.append(term + pressure if i == normal else term)
    flux.append((energy + pressure) * speed)
    stiff = GAMMA * pressure
    signal = jnp.abs(speed) + stiff * lax.rsqrt(stiff * density)
    return [density] + momentum + [energy], flux, signal


def sweep(get, put, normal, first, last):
    w, d, a, b = {}, {}, {}, {}
    prev, left = None, None
    start = first - 2
    for i in range(start, last + 4):
        w[i] = get(i)
        if i == start:
            continue
        d[i - 1] = [hi - lo for hi, lo in zip(w[i], w[i - 1])]
        m = i - 2
        if m <= start:
            continue
        a[m] = [
            clamped(0.5 * mid - (1.0 / 12.0) * (up - down), mid)
            for down, mid, up in zip(d[m - 1], d[m], d[m + 1])
        ]
        b[m + 1] = [mid - part for mid, part in zip(d[m], a[m])]
        if m < first:
            continue
        if m > first:
            lower = [v - clamped(y, 2.0 * x) for v, x, y in zip(w[m], a[m], b[m])]
            right = euler_terms(lower, normal)
            fastest = jnp.maximum(left[2], right[2])
            flux = [
                gl + gr - fastest * (ur - ul)
                for gl, gr, ul, ur in zip(left[1], right[1], left[0], right[0])
            ]
            if prev is not None:
                put(m - 1, [new - old for new, old in zip(flux, prev)])
            elif m > 0:
                put(m - 1, flux)
            prev = flux
        if m <= last:
            upper = [v + clamped(x, 2.0 * y) for v, x, y in zip(w[m], a[m], b[m])]
            left = euler_terms(upper, normal)
    if last + 1 < EDGE:
        put(last + 1, [-v for v in prev])


def y_rows(i, g):
    return pl.ds(pl.multiple_of((i % 8) * EDGE + 8 * g, 8), 8)


def own_layer(turned, direction, i, g):
    rows = pl.ds(i, 8, stride=EDGE) if direction == 0 else y_rows(i, g)
    return primitives([turned[f, g if direction == 0 else i // 8, rows, :] for f in range(FIELDS)])


def add_change(change, direction, i, g, values):
    rows = pl.ds(i, 8, stride=EDGE) if direction == 0 else y_rows(i, g)
    for f in range(FIELDS):
        at = (f, g if direction == 0 else i // 8, rows)
        change[at] = change[at] + values[f]


def inner_kernel(turned_in, after, change, turned, sem):
    load = pltpu.make_async_copy(turned_in, turned, sem)
    load.start()
    load.wait()

    def y_sweep(g, carry):
        def put(i, values):
            for f in range(FIELDS):
                change[f, i // 8, y_rows(i, g), :] = values[f]

        for i in (0, 1, EDGE - 2, EDGE - 1):
            put(i, [jnp.zeros((8, 128), F32)] * FIELDS)
        sweep(lambda i: own_layer(turned, 1, i, g), put, 1, 2, EDGE - 4)
        return carry

    lax.fori_loop(0, 4, y_sweep, 0)

    def x_sweep(g, carry):
        def put(i, values):
            add_change(change, 0, i, g, values)

        sweep(lambda i: own_layer(turned, 0, i, g), put, 0, 2, EDGE - 4)
        return carry

    lax.fori_loop(0, 4, x_sweep, 0)


def inner(turned, after):
    return pl.pallas_call(
        inner_kernel,
        out_shape=jax.ShapeDtypeStruct(TURNED_SHAPE, F32),
        in_specs=[HBM, ANY],
        out_specs=VMEM,
        scratch_shapes=[pltpu.VMEM(TURNED_SHAPE, F32), pltpu.SemaphoreType.DMA],
        compiler_params=pltpu.CompilerParams(vmem_limit_bytes=12 * MIB),
        cost_estimate=LONG,
        name="inner",
    )(held(turned), after)


def z_kernel(patches_in, z_below, z_above, partial, patches, sems):
    for k in range(SLOTS):
        pltpu.make_async_copy(patches_in.at[:, k], patches.at[:, k], sems.at[k]).start()

    def z_sweep(k, carry):
        pltpu.make_async_copy(patches_in.at[:, k], patches.at[:, k], sems.at[k]).wait()

        def get(i):
            if i < 0:
                u = [z_below[k, f, i + GHOST] for f in range(FIELDS)]
            elif i >= EDGE:
                u = [z_above[k, f, i - EDGE] for f in range(FIELDS)]
            else:
                rows = pl.ds(i % 8, 8, stride=8)
                u = [patches[f, k, i // 8, rows, :] for f in range(FIELDS)]
            return primitives(u)

        def put(i, values):
            rows = pl.ds(i % 8, 8, stride=8)
            for f in range(FIELDS):
                partial[f, k, i // 8, rows, :] = (
                    patches[f, k, i // 8, rows, :] - (0.5 * DT_DX) * values[f]
                )

        sweep(get, put, 2, -1, EDGE - 1)
        return carry

    lax.fori_loop(0, SLOTS, z_sweep, 0)


def z_update(patches, z_below, z_above):
    return pl.pallas_call(
        z_kernel,
        out_shape=jax.ShapeDtypeStruct(PATCH_SHAPE, F32),
        in_specs=[HBM, VMEM, VMEM],
        out_specs=VMEM,
        scratch_shapes=[pltpu.VMEM(PATCH_SHAPE, F32), pltpu.SemaphoreType.DMA((SLOTS,))],
        compiler_params=pltpu.CompilerParams(vmem_limit_bytes=12 * MIB),
        cost_estimate=LONG,
        name="z_update",
    )(held(patches), z_below, z_above)


def outer_kernel(place, links, turned_in, arrived, own_items, inside, partial_in, out, *scratch):
    turned, items, ghosts, change, partial, result, item_sems, sems, out_sems = scratch
    me = place[0]
    loads = [
        pltpu.make_async_copy(turned_in, turned, sems.at[0]),
        pltpu.make_async_copy(inside, change, sems.at[1]),
        pltpu.make_async_copy(partial_in, partial, sems.at[2]),
    ]
    for i in range(LINKS):
        entry = links[me * LINKS + i]
        owner = entry // SLOTS
        source = (entry % SLOTS) * 4 + (i % 4 ^ 1)
        rank = jnp.int32(0)
        for j in range(LINKS - 1):
            same = jnp.logical_and(links[owner * LINKS + j] // SLOTS == me, j < source)
            rank = rank + same.astype(jnp.int32)
        rank = jnp.minimum(rank, 1)

        @pl.when(owner != me)
        def _(i=i, owner=owner, rank=rank):
            pltpu.make_async_copy(arrived.at[owner, rank], items.at[i], item_sems.at[i]).start()

        @pl.when(owner == me)
        def _(i=i, source=source):
            pltpu.make_async_copy(own_items.at[source], items.at[i], item_sems.at[i]).start()

    for load in loads:
        load.start()
    for i in range(LINKS):
        pltpu.make_async_copy(own_items.at[i], items.at[i], item_sems.at[i]).wait()
    for side in range(4):
        for n in range(FIELDS * GHOST):
            blocks = [items[k * 4 + side, pl.ds(n * 8, 8), :] for k in range(SLOTS)]
            for g, block in enumerate(block_transpose(blocks)):
                ghosts[side, n, g] = block
    loads[0].wait()
    loads[1].wait()

    def border(g, carry):
        for direction in (1, 0):
            low, high = (0, 1) if direction == 0 else (2, 3)

            def get(i):
                if i < 0:
                    u = [ghosts[low, f * GHOST + i + GHOST, g] for f in range(FIELDS)]
                elif i >= EDGE:
                    u = [ghosts[high, f * GHOST + i - EDGE, g] for f in range(FIELDS)]
                else:
                    return own_layer(turned, direction, i, g)
                return primitives(u)

            def put(i, values):
                add_change(change, direction, i, g, values)

            sweep(get, put, direction, -1, 1)
            sweep(get, put, direction, EDGE - 3, EDGE - 1)
        return carry

    lax.fori_loop(0, 4, border, 0)
    loads[2].wait()

    for f in range(FIELDS):

        def finish(g, carry, f=f):
            for half in range(2):
                rows = pl.ds(pl.multiple_of((2 * g + half) * 8, 8), 8)
                back = jnp.transpose(change[f, g, pl.ds(half * 128, 128), :])
                for k in range(SLOTS):
                    for c in range(LAYERS):
                        n = (k * LAYERS + c) * 8
                        result[f, k, c, rows, :] = (
                            partial[f, k, c, rows, :] - (0.5 * DT_DX) * back[n : n + 8]
                        )
            return carry

        lax.fori_loop(0, 4, finish, 0)
        pltpu.make_async_copy(result.at[f], out.at[:, f], out_sems.at[f]).start()
    for f in range(FIELDS):
        pltpu.make_async_copy(result.at[f], out.at[:, f], out_sems.at[f]).wait()


def outer(place, links, turned, arrived, own_items, inside, partial):
    return pl.pallas_call(
        outer_kernel,
        out_shape=jax.ShapeDtypeStruct((SLOTS, FIELDS, LAYERS, 64, 128), F32),
        in_specs=[SMEM, SMEM] + [HBM] * 3 + [ANY] * 2,
        out_specs=HBM,
        scratch_shapes=[
            pltpu.VMEM(TURNED_SHAPE, F32),
            pltpu.VMEM((LINKS, ITEM_ROWS, 128), F32),
            pltpu.VMEM((4, FIELDS * GHOST, 4, 8, 128), F32),
            pltpu.VMEM(TURNED_SHAPE, F32),
            pltpu.VMEM(PATCH_SHAPE, F32),
            pltpu.VMEM(PATCH_SHAPE, F32),
            pltpu.SemaphoreType.DMA((LINKS,)),
            pltpu.SemaphoreType.DMA((3,)),
            pltpu.SemaphoreType.DMA((FIELDS,)),
        ],
        compiler_params=pltpu.CompilerParams(vmem_limit_bytes=24 * MIB),
        name="outer",
    )(place, links, held(turned), held(arrived), held(own_items), inside, partial)


def local(cells, moves, neighbours):
    tiled = cells.reshape(SLOTS, FIELDS, LAYERS, 8, 8, 128).transpose(0, 1, 2, 4, 3, 5)
    tiled = tiled.reshape(SLOTS, FIELDS, LAYERS, 64, 128)
    plan = moves[lax.axis_index(("gx", "gy", "gz"))].reshape(-1)
    place = lax.axis_index(("gx", "gy")).reshape(1)
    links = neighbours.reshape(-1)

    got, after = migrate(plan, tiled)
    made = ()
    for fields in GROUPS:
        received = [got[r, f] for f in fields for r in range(3)]
        made = faces(fields, plan, place, links, tiled, received, after, made)
        if not fields[0]:
            late = [got[r, f] for f in GROUPS[1] for r in range(3)]
            z_first, z_last = z_ends(plan, tiled, made[0], late)
            after = z_last
    patches, turned, send, own_items = made

    arrived = lax.all_to_all(send, ("gx", "gy"), 0, 0, tiled=True)
    layers = lax.axis_size("gz")
    up = [(i, (i + 1) % layers) for i in range(layers)]
    down = [(j, i) for i, j in up]
    z_below = lax.ppermute(z_last, "gz", up)
    z_above = lax.ppermute(z_first, "gz", down)
    partial = z_update(patches, z_below, z_above)
    inside = inner(turned, partial)
    result = outer(place, links, turned, arrived, own_items, inside, partial)
    result = result.reshape(SLOTS, FIELDS, LAYERS, 8, 8, 128).transpose(0, 1, 2, 4, 3, 5)
    return result.reshape(cells.shape)


def solution(mesh):
    return jax.shard_map(
        local,
        mesh=mesh,
        in_specs=(P(("gx", "gy", "gz"), None, None, None), P(), P()),
        out_specs=P(("gx", "gy", "gz"), None, None, None),
        check_vma=False,
    )
```

```python
import functools

import jax
import jax.numpy as jnp
from jax import lax
from jax.experimental import pallas as pl
from jax.experimental.pallas import tpu as pltpu
from jax.sharding import PartitionSpec as P

GAMMA = 5.0 / 3.0
DT_DX = 0.02
EDGE = 32
GHOST = 3
SLOTS = 4
LAYERS = 4
FIELDS = 5
PLANE = 16
LINKS = 16
GROUPS = ((0, 1, 2), (3, 4))
ITEM_ROWS = FIELDS * GHOST * 8
PATCH_SHAPE = (FIELDS, SLOTS, LAYERS, 64, 128)
PITCH = EDGE + 8
TURNED_SHAPE = (FIELDS, 4, 8 * PITCH, 128)
RIM = GHOST + 2
RIM_SHAPE = (2, 2, RIM, FIELDS, 4, 8, 128)
MIB = 1024 * 1024

F32 = jnp.float32
ANY = pl.BlockSpec(memory_space=pl.ANY)
HBM = pl.BlockSpec(memory_space=pltpu.HBM)
SMEM = pl.BlockSpec(memory_space=pltpu.SMEM)
VMEM = pl.BlockSpec(memory_space=pltpu.VMEM)
LONG = pl.CostEstimate(flops=10**12, bytes_accessed=10**10, transcendentals=10**10)
CHUNKS = (4, 4, 4, 4, 4)
STARTS = tuple(sum(CHUNKS[:c]) for c in range(len(CHUNKS)))


def held(x):
    return pltpu.with_memory_space_constraint(x, pltpu.HBM)


def start_copy(plan, slot, rounds, chunk, cells, received, target, sem, first=0, count=None):
    count = count or CHUNKS[chunk]
    taken = jnp.bool_(False)
    for r in reversed(range(rounds)):
        for j in range(2):
            hit = jnp.logical_and(plan[2 * r + j] == slot, jnp.logical_not(taken))

            @pl.when(hit)
            def _(r=r, j=j):
                source = received[r].at[j, pl.ds(first, count)]
                pltpu.make_async_copy(source, target, sem).start()

            taken = jnp.logical_or(taken, hit)

    @pl.when(jnp.logical_not(taken))
    def _():
        source = cells.at[slot, pl.ds(STARTS[chunk] + first, count)]
        pltpu.make_async_copy(source, target, sem).start()


def wait_copy(cells, count, target, sem):
    pltpu.make_async_copy(cells.at[0, pl.ds(0, count)], target, sem).wait()


def pack_kernel(sends, taken, plan, cells, *refs):
    received, refs = refs[:taken], refs[-len(sends) - 1 :]
    outs, sems = refs[:-1], refs[-1]
    at = 0
    for n, (r, c) in enumerate(sends):
        got = received[at : at + r]
        at += r
        for j in range(2):
            start_copy(plan, plan[2 * r + j], r, c, cells, got, outs[n].at[j], sems.at[n, j])
    for n, (r, c) in enumerate(sends):
        for j in range(2):
            wait_copy(cells, CHUNKS[c], outs[n].at[j], sems.at[n, j])


def pack(sends, plan, cells, received, after):
    return pl.pallas_call(
        functools.partial(pack_kernel, sends, len(received)),
        out_shape=[jax.ShapeDtypeStruct((2, CHUNKS[c], 64, 128), F32) for _, c in sends],
        in_specs=[SMEM, HBM] + [ANY] * (len(received) + len(after)),
        out_specs=[VMEM] * len(sends),
        scratch_shapes=[pltpu.SemaphoreType.DMA((len(sends), 2))],
        compiler_params=pltpu.CompilerParams(vmem_limit_bytes=4 * MIB),
        name="pack",
    )(plan, held(cells), *received, *after)


def swapped(block, axis):
    count = lax.axis_size(axis)
    return lax.ppermute(block, axis, [(i, i ^ (count // 2)) for i in range(count)])


WAVES = (
    ([(0, 0), (0, 1), (0, 2), (0, 3), (0, 4)], []),
    ([(1, 0)], []),
    ([(1, 1)], []),
    ([(1, 2), (2, 0)], []),
    ([(1, 3), (2, 1)], []),
    ([(1, 4), (2, 2)], [(2, 0)]),
    ([(2, 3)], [(2, 1)]),
    ([(2, 4)], [(2, 2)]),
)


def migrate(plan, cells):
    got, last = {}, []
    for sends, awaited in WAVES:
        received = [got[i, c] for r, c in sends for i in range(r)]
        after = list(last[-1:]) + [got[at] for at in awaited]
        last = pack(sends, plan, cells, received, after)
        for (r, c), block in zip(sends, last):
            got[r, c] = swapped(block, ("gx", "gy", "gz")[r])
    return got, last[-1]


def primitives(u):
    inv = 1.0 / u[0]
    v = [u[i] * inv for i in (1, 2, 3)]
    kinetic = u[1] * v[0] + u[2] * v[1] + u[3] * v[2]
    return [u[0]] + v + [(GAMMA - 1.0) * (u[4] - 0.5 * kinetic)]


def block_transpose(b):
    lane = lax.broadcasted_iota(jnp.int32, b[0].shape, 1)
    low = lane < 64
    even = (lane & 32) == 0

    def rolled(x, shift):
        return pltpu.roll(x, shift, 1)

    a0 = jnp.where(low, b[0], rolled(b[2], 64))
    a2 = jnp.where(low, rolled(b[0], 64), b[2])
    a1 = jnp.where(low, b[1], rolled(b[3], 64))
    a3 = jnp.where(low, rolled(b[1], 64), b[3])
    return [
        jnp.where(even, a0, rolled(a1, 32)),
        jnp.where(even, rolled(a0, 96), a1),
        jnp.where(even, a2, rolled(a3, 32)),
        jnp.where(even, rolled(a2, 96), a3),
    ]


def y_rows(i, g):
    return pl.ds(pl.multiple_of((i % 8) * PITCH + 8 * g, 8), 8)


def turned_rows(direction, i, g):
    if direction == 0:
        return g, pl.ds(i, 8, stride=PITCH)
    return i // 8, y_rows(i, g)


def flat(turned, f):
    rows = [turned[f, g, pl.ds(y * PITCH, EDGE), :] for g in range(4) for y in range(8)]
    return jnp.concatenate(rows, axis=0)


def pieces(f):
    out = []
    for c, start in enumerate(STARTS):
        low, high = max(start, f * LAYERS), min(start + CHUNKS[c], (f + 1) * LAYERS)
        if low < high:
            out.append((c, low - start, high - low, low - f * LAYERS))
    return out


def chunks_of(fields):
    return sorted({c for f in fields for c, _, _, _ in pieces(f)})


def faces_kernel(fields, plan, place, links, cells, *refs):
    count, first, last = len(fields), fields[0], fields[0] > 0
    chunks = chunks_of(fields)
    received = refs[: 3 * len(chunks)]
    refs = refs[3 * len(chunks) + 1 + 4 * last :]
    patches_out, turned_out, send, own_items = refs[:4]
    patches, turned, items, sems, item_sems, out_sems = refs[-6:]
    parts = []
    for n, f in enumerate(fields):
        for p, (c, start, size, layer) in enumerate(pieces(f)):
            got = received[3 * chunks.index(c) : 3 * chunks.index(c) + 3]
            for k in range(SLOTS):
                target, sem = patches.at[n, k, pl.ds(layer, size)], sems.at[n, k, p]
                start_copy(plan, k, 3, c, cells, got, target, sem, start, size)
                parts.append((n, size, target, sem))
    loads = []
    if last:
        z_first, z_last, ends, end_sems = refs[4:8]
        for end, c in ((0, 0), (1, LAYERS - 1)):
            source = patches_out.at[pl.ds(0, first), :, c]
            loads.append(pltpu.make_async_copy(source, ends.at[end], end_sems.at[end]))
    for load in loads:
        load.start()

    mine = pl.ds(first, count)
    outs = [
        pltpu.make_async_copy(patches, patches_out.at[mine], out_sems.at[0]),
        pltpu.make_async_copy(turned, turned_out.at[mine], out_sems.at[1]),
    ]
    for n, f in enumerate(fields):
        for at, size, target, sem in parts:
            if at == n:
                wait_copy(cells, size, target, sem)
        columns = [
            jnp.concatenate(
                [patches[n, k, c, pl.ds(8 * b, 8), :] for k in range(SLOTS) for c in range(LAYERS)],
                axis=0,
            )
            for b in range(8)
        ]
        rows = jnp.transpose(jnp.concatenate(columns, axis=1))
        for y in range(EDGE):
            turned[n, y // 8, pl.ds(y % 8 * PITCH, EDGE), :] = rows[y * EDGE : (y + 1) * EDGE]
    for copy in outs:
        copy.start()

    me = place[0]
    owners = [links[me * LINKS + i] // SLOTS for i in range(LINKS)]
    rows = pl.ds(first * GHOST * 8, count * GHOST * 8)
    for side in range(4):
        start = EDGE - GHOST if side % 2 else 0
        blocks = []
        for g in range(4):
            tiles = []
            for n in range(count):
                for layer in range(start, start + GHOST):
                    block, where = turned_rows(side // 2, layer, g)
                    tiles.append(turned[n, block, where, :])
            blocks.append(jnp.concatenate(tiles, axis=0))
        for k, block in enumerate(block_transpose(blocks)):
            items[k * 4 + side] = block
        for i in range(side, LINKS, 4):
            rank = jnp.int32(0)
            for j in range(i):
                rank = rank + (owners[j] == owners[i]).astype(jnp.int32)
            rank = jnp.minimum(rank, 1)

            @pl.when(owners[i] != me)
            def _(i=i, rank=rank):
                target = send.at[owners[i], rank, rows]
                pltpu.make_async_copy(items.at[i], target, item_sems.at[i]).start()

            @pl.when(owners[i] == me)
            def _(i=i):
                target = own_items.at[i, rows]
                pltpu.make_async_copy(items.at[i], target, item_sems.at[i]).start()

    for load in loads:
        load.wait()
    if last:
        for f in range(FIELDS):
            for k in range(SLOTS):
                if f < first:
                    head, tail = ends.at[0, f, k], ends.at[1, f, k]
                else:
                    head, tail = patches.at[f - first, k, 0], patches.at[f - first, k, LAYERS - 1]
                for layer in range(GHOST):
                    z_first[k, f, layer] = head[pl.ds(layer, 8, stride=8), :]
                    z_last[k, f, layer] = tail[pl.ds(8 - GHOST + layer, 8, stride=8), :]

    for i in range(LINKS):
        pltpu.make_async_copy(items.at[i], own_items.at[i, rows], item_sems.at[i]).wait()
    for copy in outs:
        copy.wait()


def faces(fields, plan, place, links, cells, received, after, carried):
    count, first, last = len(fields), fields[0], fields[0] > 0
    held_chunks = 3 * len(chunks_of(fields))
    z_shape = jax.ShapeDtypeStruct((SLOTS, FIELDS, GHOST, 8, 128), F32)
    scratch = [
        pltpu.VMEM((count,) + PATCH_SHAPE[1:], F32),
        pltpu.VMEM((count,) + TURNED_SHAPE[1:], F32),
        pltpu.VMEM((LINKS, count * GHOST * 8, 128), F32),
        pltpu.SemaphoreType.DMA((count, SLOTS, 2)),
        pltpu.SemaphoreType.DMA((LINKS,)),
        pltpu.SemaphoreType.DMA((2,)),
    ]
    if last:
        scratch = [
            pltpu.VMEM((2, first, SLOTS, 64, 128), F32),
            pltpu.SemaphoreType.DMA((2,)),
        ] + scratch
    inputs = [held(cells)] + list(received) + [after] + [held(x) for x in carried]
    return pl.pallas_call(
        functools.partial(faces_kernel, fields),
        out_shape=[
            pltpu.HBM(PATCH_SHAPE, F32),
            pltpu.HBM(TURNED_SHAPE, F32),
            pltpu.HBM((PLANE, 2, ITEM_ROWS, 128), F32),
            pltpu.HBM((LINKS, ITEM_ROWS, 128), F32),
        ]
        + [z_shape] * (2 * last),
        in_specs=[SMEM] * 3 + [HBM] + [ANY] * (held_chunks + 1) + [HBM] * len(carried),
        out_specs=[HBM] * 4 + [VMEM] * (2 * last),
        scratch_shapes=scratch,
        input_output_aliases={held_chunks + 5 + i: i for i in range(len(carried))},
        compiler_params=pltpu.CompilerParams(vmem_limit_bytes=16 * MIB),
        cost_estimate=LONG if last else None,
        name="faces",
    )(plan, place, links, *inputs)


def clamped(x, y):
    return jnp.minimum(jnp.maximum(x, jnp.minimum(y, 0.0)), jnp.maximum(y, 0.0))


def euler_terms(w, normal):
    density, velocity, pressure = w[0], w[1:4], w[4]
    speed = velocity[normal]
    momentum = [density * v for v in velocity]
    kinetic = momentum[0] * velocity[0] + momentum[1] * velocity[1] + momentum[2] * velocity[2]
    energy = 1.5 * pressure + 0.5 * kinetic
    flux = [momentum[normal]]
    for i in range(3):
        term = momentum[i] * speed
        flux.append(term + pressure if i == normal else term)
    flux.append((energy + pressure) * speed)
    stiff = GAMMA * pressure
    signal = jnp.abs(speed) + stiff * lax.rsqrt(stiff * density)
    return [density] + momentum + [energy], flux, signal


def sweep(get, put, normal, first, last):
    w, d, a, b = {}, {}, {}, {}
    prev, left = None, None
    start = first - 2
    for i in range(start, last + 4):
        w[i] = get(i)
        if i == start:
            continue
        d[i - 1] = [hi - lo for hi, lo in zip(w[i], w[i - 1])]
        m = i - 2
        if m <= start:
            continue
        a[m] = [
            clamped(0.5 * mid - (1.0 / 12.0) * (up - down), mid)
            for down, mid, up in zip(d[m - 1], d[m], d[m + 1])
        ]
        b[m + 1] = [mid - part for mid, part in zip(d[m], a[m])]
        if m < first:
            continue
        if m > first:
            lower = [v - clamped(y, 2.0 * x) for v, x, y in zip(w[m], a[m], b[m])]
            right = euler_terms(lower, normal)
            fastest = jnp.maximum(left[2], right[2])
            flux = [
                gl + gr - fastest * (ur - ul)
                for gl, gr, ul, ur in zip(left[1], right[1], left[0], right[0])
            ]
            if prev is not None:
                put(m - 1, [new - old for new, old in zip(flux, prev)])
            elif m > 0:
                put(m - 1, flux)
            prev = flux
        if m <= last:
            upper = [v + clamped(x, 2.0 * y) for v, x, y in zip(w[m], a[m], b[m])]
            left = euler_terms(upper, normal)
    if last + 1 < EDGE:
        put(last + 1, [-v for v in prev])


def inner_kernel(turned_in, patches_in, z_below, z_above, out, rim_out, *scratch):
    turned, patches, change, partial, rim, sems, out_sems = scratch
    loads = [
        pltpu.make_async_copy(patches_in.at[:, k], patches.at[:, k], sems.at[k])
        for k in range(SLOTS)
    ]
    loads.append(pltpu.make_async_copy(turned_in, turned, sems.at[SLOTS]))
    for load in loads:
        load.start()
    for load in loads[:SLOTS]:
        load.wait()

    def z_sweep(k, carry):
        def get(i):
            if i < 0:
                u = [z_below[k, f, i + GHOST] for f in range(FIELDS)]
            elif i >= EDGE:
                u = [z_above[k, f, i - EDGE] for f in range(FIELDS)]
            else:
                rows = pl.ds(i % 8, 8, stride=8)
                u = [patches[f, k, i // 8, rows, :] for f in range(FIELDS)]
            return primitives(u)

        def put(i, values):
            rows = pl.ds(i % 8, 8, stride=8)
            for f in range(FIELDS):
                partial[f, k, i // 8, rows, :] = (
                    patches[f, k, i // 8, rows, :] - (0.5 * DT_DX) * values[f]
                )

        sweep(get, put, 2, -1, EDGE - 1)
        return carry

    lax.fori_loop(0, SLOTS, z_sweep, 0)
    loads[SLOTS].wait()

    def plane_sweep(direction, g, put):
        def get(i):
            block, rows = turned_rows(direction, i, g)
            w = primitives([turned[f, block, rows, :] for f in range(FIELDS)])
            end, at = (0, i) if i < RIM else (1, i - EDGE + RIM)
            if 0 <= at < RIM:
                for f in range(FIELDS):
                    rim[direction, end, at, f, g] = w[f]
            return w

        sweep(get, put, direction, 2, EDGE - 4)

    def y_sweep(g, carry):
        def put(i, values):
            block, rows = turned_rows(1, i, g)
            for f in range(FIELDS):
                change[f, block, rows, :] = values[f]

        for i in (0, 1, EDGE - 2, EDGE - 1):
            put(i, [jnp.zeros((8, 128), F32)] * FIELDS)
        plane_sweep(1, g, put)
        return carry

    lax.fori_loop(0, 4, y_sweep, 0)

    def x_sweep(g, carry):
        def put(i, values):
            block, rows = turned_rows(0, i, g)
            for f in range(FIELDS):
                change[f, block, rows, :] = change[f, block, rows, :] + values[f]

        plane_sweep(0, g, put)
        return carry

    lax.fori_loop(0, 4, x_sweep, 0)
    rim_copy = pltpu.make_async_copy(rim, rim_out, out_sems.at[FIELDS])
    rim_copy.start()
    copies = []
    for f in range(FIELDS):
        add_turned(change, partial, f, partial.at[f])
        copies.append(pltpu.make_async_copy(partial.at[f], out.at[f], out_sems.at[f]))
        copies[f].start()
    for copy in copies + [rim_copy]:
        copy.wait()


def add_turned(change, partial, f, result):
    back = (0.5 * DT_DX) * jnp.transpose(flat(change, f))
    for k in range(SLOTS):
        for c in range(LAYERS):
            n = (k * LAYERS + c) * 8
            for b in range(8):
                rows = pl.ds(8 * b, 8)
                result[k, c, rows, :] = (
                    partial[f, k, c, rows, :] - back[n : n + 8, 128 * b : 128 * (b + 1)]
                )


def inner(turned, patches, z_below, z_above):
    return pl.pallas_call(
        inner_kernel,
        out_shape=[pltpu.HBM(PATCH_SHAPE, F32), pltpu.HBM(RIM_SHAPE, F32)],
        in_specs=[HBM, HBM, VMEM, VMEM],
        out_specs=[HBM, HBM],
        scratch_shapes=[
            pltpu.VMEM(TURNED_SHAPE, F32),
            pltpu.VMEM(PATCH_SHAPE, F32),
            pltpu.VMEM(TURNED_SHAPE, F32),
            pltpu.VMEM(PATCH_SHAPE, F32),
            pltpu.VMEM(RIM_SHAPE, F32),
            pltpu.SemaphoreType.DMA((SLOTS + 1,)),
            pltpu.SemaphoreType.DMA((FIELDS + 1,)),
        ],
        compiler_params=pltpu.CompilerParams(vmem_limit_bytes=24 * MIB),
        cost_estimate=LONG,
        name="inner",
    )(held(turned), held(patches), z_below, z_above)


def outer_kernel(place, links, rim_in, arrived, own_items, partial_in, out, *scratch):
    rim, items, ghosts, change, partial, result, item_sems, sems, out_sems = scratch
    me = place[0]
    for i in range(LINKS):
        entry = links[me * LINKS + i]
        owner = entry // SLOTS
        source = (entry % SLOTS) * 4 + (i % 4 ^ 1)
        rank = jnp.int32(0)
        for j in range(LINKS - 1):
            same = jnp.logical_and(links[owner * LINKS + j] // SLOTS == me, j < source)
            rank = rank + same.astype(jnp.int32)
        rank = jnp.minimum(rank, 1)

        @pl.when(owner != me)
        def _(i=i, owner=owner, rank=rank):
            pltpu.make_async_copy(arrived.at[owner, rank], items.at[i], item_sems.at[i]).start()

        @pl.when(owner == me)
        def _(i=i, source=source):
            pltpu.make_async_copy(own_items.at[source], items.at[i], item_sems.at[i]).start()

    loads = [
        pltpu.make_async_copy(rim_in, rim, sems.at[0]),
        pltpu.make_async_copy(partial_in, partial, sems.at[1]),
    ]
    for load in loads:
        load.start()
    change[...] = jnp.zeros(TURNED_SHAPE, F32)
    for i in range(LINKS):
        pltpu.make_async_copy(own_items.at[i], items.at[i], item_sems.at[i]).wait()
    for side in range(4):
        blocks = [items[k * 4 + side] for k in range(SLOTS)]
        for g, block in enumerate(block_transpose(blocks)):
            ghosts[side, g] = block
    loads[0].wait()

    def border(g, carry):
        for direction in (1, 0):

            def get(i):
                if 0 <= i < EDGE:
                    end, at = (0, i) if i < RIM else (1, i - EDGE + RIM)
                    return [rim[direction, end, at, f, g] for f in range(FIELDS)]
                side, layer = (0, i + GHOST) if i < 0 else (1, i - EDGE)
                rows = [pl.ds((f * GHOST + layer) * 8, 8) for f in range(FIELDS)]
                return primitives([ghosts[2 * direction + side, g, at, :] for at in rows])

            def put(i, values):
                block, rows = turned_rows(direction, i, g)
                for f in range(FIELDS):
                    change[f, block, rows, :] = change[f, block, rows, :] + values[f]

            sweep(get, put, direction, -1, 1)
            sweep(get, put, direction, EDGE - 3, EDGE - 1)
        return carry

    lax.fori_loop(0, 4, border, 0)
    loads[1].wait()
    copies = []
    for f in range(FIELDS):
        add_turned(change, partial, f, result.at[f])
        copies.append(pltpu.make_async_copy(result.at[f], out.at[:, f], out_sems.at[f]))
        copies[f].start()
    for copy in copies:
        copy.wait()


def outer(place, links, rim, arrived, own_items, partial):
    return pl.pallas_call(
        outer_kernel,
        out_shape=jax.ShapeDtypeStruct((SLOTS, FIELDS, LAYERS, 64, 128), F32),
        in_specs=[SMEM, SMEM] + [HBM] * 4,
        out_specs=HBM,
        scratch_shapes=[
            pltpu.VMEM(RIM_SHAPE, F32),
            pltpu.VMEM((LINKS, ITEM_ROWS, 128), F32),
            pltpu.VMEM((4, 4, ITEM_ROWS, 128), F32),
            pltpu.VMEM(TURNED_SHAPE, F32),
            pltpu.VMEM(PATCH_SHAPE, F32),
            pltpu.VMEM(PATCH_SHAPE, F32),
            pltpu.SemaphoreType.DMA((LINKS,)),
            pltpu.SemaphoreType.DMA((2,)),
            pltpu.SemaphoreType.DMA((FIELDS,)),
        ],
        compiler_params=pltpu.CompilerParams(vmem_limit_bytes=24 * MIB),
        name="outer",
    )(place, links, held(rim), held(arrived), held(own_items), held(partial))


def local(cells, moves, neighbours):
    tiled = cells.reshape(SLOTS, FIELDS, LAYERS, 8, 8, 128).transpose(0, 1, 2, 4, 3, 5)
    tiled = tiled.reshape(SLOTS, FIELDS * LAYERS, 64, 128)
    plan = moves[lax.axis_index(("gx", "gy", "gz"))].reshape(-1)
    place = lax.axis_index(("gx", "gy")).reshape(1)
    links = neighbours.reshape(-1)

    got, after = migrate(plan, tiled)
    made = ()
    for fields in GROUPS:
        received = [got[r, c] for c in chunks_of(fields) for r in range(3)]
        made = faces(fields, plan, place, links, tiled, received, after, made)
    patches, turned, send, own_items, z_first, z_last = made

    arrived = lax.all_to_all(send, ("gx", "gy"), 0, 0, tiled=True)
    layers = lax.axis_size("gz")
    up = [(i, (i + 1) % layers) for i in range(layers)]
    down = [(j, i) for i, j in up]
    z_below = lax.ppermute(z_last, "gz", up)
    z_above = lax.ppermute(z_first, "gz", down)
    partial, rim = inner(turned, patches, z_below, z_above)
    result = outer(place, links, rim, arrived, own_items, partial)
    result = result.reshape(SLOTS, FIELDS, LAYERS, 8, 8, 128).transpose(0, 1, 2, 4, 3, 5)
    return result.reshape(cells.shape)


def solution(mesh):
    return jax.shard_map(
        local,
        mesh=mesh,
        in_specs=(P(("gx", "gy", "gz"), None, None, None), P(), P()),
        out_specs=P(("gx", "gy", "gz"), None, None, None),
        check_vma=False,
    )
```

```python
import functools

import jax
import jax.numpy as jnp
from jax import lax
from jax.experimental import pallas as pl
from jax.experimental.pallas import tpu as pltpu
from jax.sharding import PartitionSpec as P

GAMMA = 5.0 / 3.0
DT_DX = 0.02
EDGE = 32
GHOST = 3
SLOTS = 4
LAYERS = 4
FIELDS = 5
PLANE = 16
LINKS = 16
GROUPS = ((0, 1, 2), (3, 4))
ITEM_ROWS = FIELDS * GHOST * 8
PATCH_SHAPE = (FIELDS, SLOTS, LAYERS, 64, 128)
PITCH = EDGE + 8
TURNED_SHAPE = (FIELDS, 4, 8 * PITCH, 128)
RIM = GHOST + 2
RIM_SHAPE = (2, 2, RIM, FIELDS, 4, 8, 128)
MIB = 1024 * 1024

F32 = jnp.float32
ANY = pl.BlockSpec(memory_space=pl.ANY)
HBM = pl.BlockSpec(memory_space=pltpu.HBM)
SMEM = pl.BlockSpec(memory_space=pltpu.SMEM)
VMEM = pl.BlockSpec(memory_space=pltpu.VMEM)
LONG = pl.CostEstimate(flops=10**12, bytes_accessed=10**10, transcendentals=10**10)
CHUNKS = (4, 4, 4, 4, 4)
STARTS = tuple(sum(CHUNKS[:c]) for c in range(len(CHUNKS)))


def held(x):
    return pltpu.with_memory_space_constraint(x, pltpu.HBM)


def start_copies(plan, slot, rounds, cells, jobs):
    taken = jnp.bool_(False)
    for r in reversed(range(rounds)):
        for j in range(2):
            hit = jnp.logical_and(plan[2 * r + j] == slot, jnp.logical_not(taken))

            @pl.when(hit)
            def _(r=r, j=j):
                for _, received, first, count, target, sem in jobs:
                    source = received[r].at[j, pl.ds(first, count)]
                    pltpu.make_async_copy(source, target, sem).start()

            taken = jnp.logical_or(taken, hit)

    @pl.when(jnp.logical_not(taken))
    def _():
        for chunk, _, first, count, target, sem in jobs:
            source = cells.at[slot, pl.ds(STARTS[chunk] + first, count)]
            pltpu.make_async_copy(source, target, sem).start()


def wait_copy(cells, count, target, sem):
    pltpu.make_async_copy(cells.at[0, pl.ds(0, count)], target, sem).wait()


def pack_kernel(sends, taken, plan, cells, *refs):
    received, refs = refs[:taken], refs[-len(sends) - 1 :]
    outs, sems = refs[:-1], refs[-1]
    at = 0
    for n, (r, c) in enumerate(sends):
        got = received[at : at + r]
        at += r
        for j in range(2):
            job = (c, got, 0, CHUNKS[c], outs[n].at[j], sems.at[n, j])
            start_copies(plan, plan[2 * r + j], r, cells, [job])
    for n, (r, c) in enumerate(sends):
        for j in range(2):
            wait_copy(cells, CHUNKS[c], outs[n].at[j], sems.at[n, j])


def pack(sends, plan, cells, received, after):
    return pl.pallas_call(
        functools.partial(pack_kernel, sends, len(received)),
        out_shape=[jax.ShapeDtypeStruct((2, CHUNKS[c], 64, 128), F32) for _, c in sends],
        in_specs=[SMEM, HBM] + [ANY] * (len(received) + len(after)),
        out_specs=[VMEM] * len(sends),
        scratch_shapes=[pltpu.SemaphoreType.DMA((len(sends), 2))],
        compiler_params=pltpu.CompilerParams(vmem_limit_bytes=4 * MIB),
        name="pack",
    )(plan, held(cells), *received, *after)


def swapped(block, axis):
    count = lax.axis_size(axis)
    return lax.ppermute(block, axis, [(i, i ^ (count // 2)) for i in range(count)])


WAVES = (
    ([(0, 0), (0, 1), (0, 2), (0, 3), (0, 4)], []),
    ([(1, 0)], []),
    ([(1, 1)], []),
    ([(1, 2), (2, 0)], []),
    ([(1, 3), (2, 1)], []),
    ([(1, 4), (2, 2)], [(2, 0)]),
    ([(2, 3)], [(2, 1)]),
    ([(2, 4)], [(2, 2)]),
)


def migrate(plan, cells):
    got, last = {}, []
    for sends, awaited in WAVES:
        received = [got[i, c] for r, c in sends for i in range(r)]
        after = list(last[-1:]) + [got[at] for at in awaited]
        last = pack(sends, plan, cells, received, after)
        for (r, c), block in zip(sends, last):
            got[r, c] = swapped(block, ("gx", "gy", "gz")[r])
    return got, last[-1]


def primitives(u):
    inv = 1.0 / u[0]
    v = [u[i] * inv for i in (1, 2, 3)]
    kinetic = u[1] * v[0] + u[2] * v[1] + u[3] * v[2]
    return [u[0]] + v + [(GAMMA - 1.0) * (u[4] - 0.5 * kinetic)]


def block_transpose(b):
    lane = lax.broadcasted_iota(jnp.int32, b[0].shape, 1)
    low = lane < 64
    even = (lane & 32) == 0

    def rolled(x, shift):
        return pltpu.roll(x, shift, 1)

    a0 = jnp.where(low, b[0], rolled(b[2], 64))
    a2 = jnp.where(low, rolled(b[0], 64), b[2])
    a1 = jnp.where(low, b[1], rolled(b[3], 64))
    a3 = jnp.where(low, rolled(b[1], 64), b[3])
    return [
        jnp.where(even, a0, rolled(a1, 32)),
        jnp.where(even, rolled(a0, 96), a1),
        jnp.where(even, a2, rolled(a3, 32)),
        jnp.where(even, rolled(a2, 96), a3),
    ]


def y_rows(i, g):
    return pl.ds(pl.multiple_of((i % 8) * PITCH + 8 * g, 8), 8)


def turned_rows(direction, i, g):
    if direction == 0:
        return g, pl.ds(i, 8, stride=PITCH)
    return i // 8, y_rows(i, g)


def flat(turned, f):
    rows = [turned[f, g, pl.ds(y * PITCH, EDGE), :] for g in range(4) for y in range(8)]
    return jnp.concatenate(rows, axis=0)


def turn(patches, turned, n):
    columns = [
        jnp.concatenate(
            [patches[n, k, c, pl.ds(8 * b, 8), :] for k in range(SLOTS) for c in range(LAYERS)],
            axis=0,
        )
        for b in range(8)
    ]
    rows = jnp.transpose(jnp.concatenate(columns, axis=1))
    for y in range(EDGE):
        turned[n, y // 8, pl.ds(y % 8 * PITCH, EDGE), :] = rows[y * EDGE : (y + 1) * EDGE]


def pieces(f):
    out = []
    for c, start in enumerate(STARTS):
        low, high = max(start, f * LAYERS), min(start + CHUNKS[c], (f + 1) * LAYERS)
        if low < high:
            out.append((c, low - start, high - low, low - f * LAYERS))
    return out


def chunks_of(fields):
    return sorted({c for f in fields for c, _, _, _ in pieces(f)})


def faces_kernel(fields, plan, place, links, cells, *refs):
    count, first, last = len(fields), fields[0], fields[0] > 0
    chunks = chunks_of(fields)
    received = refs[: 3 * len(chunks)]
    refs = refs[3 * len(chunks) + 1 + 3 * last :]
    patches_out, send, own_items = refs[:3]
    patches, turned, items, sems, item_sems, out_sem = refs[-6:]
    parts = []
    for k in range(SLOTS):
        jobs = []
        for n, f in enumerate(fields):
            for p, (c, start, size, layer) in enumerate(pieces(f)):
                got = received[3 * chunks.index(c) : 3 * chunks.index(c) + 3]
                target, sem = patches.at[n, k, pl.ds(layer, size)], sems.at[n, k, p]
                jobs.append((c, got, start, size, target, sem))
                parts.append((n, size, target, sem))
        start_copies(plan, k, 3, cells, jobs)
    loads = []
    if last:
        z_first, z_last, ends, end_sems = refs[3:7]
        for end, c in ((0, 0), (1, LAYERS - 1)):
            source = patches_out.at[pl.ds(0, first), :, c]
            loads.append(pltpu.make_async_copy(source, ends.at[end], end_sems.at[end]))
    for load in loads:
        load.start()

    whole = pltpu.make_async_copy(patches, patches_out.at[pl.ds(first, count)], out_sem)
    for n, f in enumerate(fields):
        for at, size, target, sem in parts:
            if at == n:
                wait_copy(cells, size, target, sem)
        turn(patches, turned, n)
    whole.start()

    me = place[0]
    owners = [links[me * LINKS + i] // SLOTS for i in range(LINKS)]
    rows = pl.ds(first * GHOST * 8, count * GHOST * 8)
    for side in range(4):
        start = EDGE - GHOST if side % 2 else 0
        blocks = []
        for g in range(4):
            tiles = []
            for n in range(count):
                for layer in range(start, start + GHOST):
                    block, where = turned_rows(side // 2, layer, g)
                    tiles.append(turned[n, block, where, :])
            blocks.append(jnp.concatenate(tiles, axis=0))
        for k, block in enumerate(block_transpose(blocks)):
            items[k * 4 + side] = block
        for i in range(side, LINKS, 4):
            rank = jnp.int32(0)
            for j in range(i):
                rank = rank + (owners[j] == owners[i]).astype(jnp.int32)
            rank = jnp.minimum(rank, 1)

            @pl.when(owners[i] != me)
            def _(i=i, rank=rank):
                target = send.at[owners[i], rank, rows]
                pltpu.make_async_copy(items.at[i], target, item_sems.at[i]).start()

            @pl.when(owners[i] == me)
            def _(i=i):
                target = own_items.at[i, rows]
                pltpu.make_async_copy(items.at[i], target, item_sems.at[i]).start()

    for load in loads:
        load.wait()
    if last:
        for f in range(FIELDS):
            for k in range(SLOTS):
                if f < first:
                    head, tail = ends.at[0, f, k], ends.at[1, f, k]
                else:
                    head, tail = patches.at[f - first, k, 0], patches.at[f - first, k, LAYERS - 1]
                for layer in range(GHOST):
                    z_first[k, f, layer] = head[pl.ds(layer, 8, stride=8), :]
                    z_last[k, f, layer] = tail[pl.ds(8 - GHOST + layer, 8, stride=8), :]

    for i in range(LINKS):
        pltpu.make_async_copy(items.at[i], own_items.at[i, rows], item_sems.at[i]).wait()
    whole.wait()


def faces(fields, plan, place, links, cells, received, after, carried):
    count, first, last = len(fields), fields[0], fields[0] > 0
    held_chunks = 3 * len(chunks_of(fields))
    z_shape = jax.ShapeDtypeStruct((SLOTS, FIELDS, GHOST, 8, 128), F32)
    scratch = [
        pltpu.VMEM((count,) + PATCH_SHAPE[1:], F32),
        pltpu.VMEM((count,) + TURNED_SHAPE[1:], F32),
        pltpu.VMEM((LINKS, count * GHOST * 8, 128), F32),
        pltpu.SemaphoreType.DMA((count, SLOTS, 2)),
        pltpu.SemaphoreType.DMA((LINKS,)),
        pltpu.SemaphoreType.DMA,
    ]
    if last:
        scratch = [
            pltpu.VMEM((2, first, SLOTS, 64, 128), F32),
            pltpu.SemaphoreType.DMA((2,)),
        ] + scratch
    inputs = [held(cells)] + list(received) + [after] + [held(x) for x in carried]
    return pl.pallas_call(
        functools.partial(faces_kernel, fields),
        out_shape=[
            pltpu.HBM(PATCH_SHAPE, F32),
            pltpu.HBM((PLANE, 2, ITEM_ROWS, 128), F32),
            pltpu.HBM((LINKS, ITEM_ROWS, 128), F32),
        ]
        + [z_shape] * (2 * last),
        in_specs=[SMEM] * 3 + [HBM] + [ANY] * (held_chunks + 1) + [HBM] * len(carried),
        out_specs=[HBM] * 3 + [VMEM] * (2 * last),
        scratch_shapes=scratch,
        input_output_aliases={held_chunks + 5 + i: i for i in range(len(carried))},
        compiler_params=pltpu.CompilerParams(vmem_limit_bytes=16 * MIB),
        cost_estimate=LONG if last else None,
        name="faces",
    )(plan, place, links, *inputs)


def clamped(x, y):
    return jnp.minimum(jnp.maximum(x, jnp.minimum(y, 0.0)), jnp.maximum(y, 0.0))


def euler_terms(w, normal):
    density, velocity, pressure = w[0], w[1:4], w[4]
    speed = velocity[normal]
    momentum = [density * v for v in velocity]
    kinetic = momentum[0] * velocity[0] + momentum[1] * velocity[1] + momentum[2] * velocity[2]
    energy = 1.5 * pressure + 0.5 * kinetic
    flux = [momentum[normal]]
    for i in range(3):
        term = momentum[i] * speed
        flux.append(term + pressure if i == normal else term)
    flux.append((energy + pressure) * speed)
    stiff = GAMMA * pressure
    signal = jnp.abs(speed) + stiff * lax.rsqrt(stiff * density)
    return [density] + momentum + [energy], flux, signal


def sweep(get, put, normal, first, last):
    w, d, a, b = {}, {}, {}, {}
    prev, left = None, None
    start = first - 2
    for i in range(start, last + 4):
        w[i] = get(i)
        if i == start:
            continue
        d[i - 1] = [hi - lo for hi, lo in zip(w[i], w[i - 1])]
        m = i - 2
        if m <= start:
            continue
        a[m] = [
            clamped(0.5 * mid - (1.0 / 12.0) * (up - down), mid)
            for down, mid, up in zip(d[m - 1], d[m], d[m + 1])
        ]
        b[m + 1] = [mid - part for mid, part in zip(d[m], a[m])]
        if m < first:
            continue
        if m > first:
            lower = [v - clamped(y, 2.0 * x) for v, x, y in zip(w[m], a[m], b[m])]
            right = euler_terms(lower, normal)
            fastest = jnp.maximum(left[2], right[2])
            flux = [
                gl + gr - fastest * (ur - ul)
                for gl, gr, ul, ur in zip(left[1], right[1], left[0], right[0])
            ]
            if prev is not None:
                put(m - 1, [new - old for new, old in zip(flux, prev)])
            elif m > 0:
                put(m - 1, flux)
            prev = flux
        if m <= last:
            upper = [v + clamped(x, 2.0 * y) for v, x, y in zip(w[m], a[m], b[m])]
            left = euler_terms(upper, normal)
    if last + 1 < EDGE:
        put(last + 1, [-v for v in prev])


def inner_kernel(place, links, patches_in, z_below, z_above, out, rim_out, table, *scratch):
    turned, patches, change, partial, rim, sems, out_sems = scratch
    loads = [
        pltpu.make_async_copy(patches_in.at[:, k], patches.at[:, k], sems.at[k])
        for k in range(SLOTS)
    ]
    for load in loads:
        load.start()
    me = place[0]
    for i in range(LINKS):
        entry = links[me * LINKS + i]
        owner = entry // SLOTS
        source = (entry % SLOTS) * 4 + (i % 4 ^ 1)
        rank = jnp.int32(0)
        for j in range(LINKS - 1):
            same = jnp.logical_and(links[owner * LINKS + j] // SLOTS == me, j < source)
            rank = rank + same.astype(jnp.int32)
        table[i] = owner
        table[LINKS + i] = jnp.minimum(rank, 1)
        table[2 * LINKS + i] = source
    for load in loads:
        load.wait()
    for f in range(FIELDS):
        turn(patches, turned, f)

    def z_sweep(k, carry):
        def get(i):
            if i < 0:
                u = [z_below[k, f, i + GHOST] for f in range(FIELDS)]
            elif i >= EDGE:
                u = [z_above[k, f, i - EDGE] for f in range(FIELDS)]
            else:
                rows = pl.ds(i % 8, 8, stride=8)
                u = [patches[f, k, i // 8, rows, :] for f in range(FIELDS)]
            return primitives(u)

        def put(i, values):
            rows = pl.ds(i % 8, 8, stride=8)
            for f in range(FIELDS):
                partial[f, k, i // 8, rows, :] = (
                    patches[f, k, i // 8, rows, :] - (0.5 * DT_DX) * values[f]
                )

        sweep(get, put, 2, -1, EDGE - 1)
        return carry

    lax.fori_loop(0, SLOTS, z_sweep, 0)

    def plane_sweep(direction, g, put):
        def get(i):
            block, rows = turned_rows(direction, i, g)
            w = primitives([turned[f, block, rows, :] for f in range(FIELDS)])
            end, at = (0, i) if i < RIM else (1, i - EDGE + RIM)
            if 0 <= at < RIM:
                for f in range(FIELDS):
                    rim[direction, end, at, f, g] = w[f]
            return w

        sweep(get, put, direction, 2, EDGE - 4)

    def y_sweep(g, carry):
        def put(i, values):
            block, rows = turned_rows(1, i, g)
            for f in range(FIELDS):
                change[f, block, rows, :] = values[f]

        for i in (0, 1, EDGE - 2, EDGE - 1):
            put(i, [jnp.zeros((8, 128), F32)] * FIELDS)
        plane_sweep(1, g, put)
        return carry

    lax.fori_loop(0, 4, y_sweep, 0)

    def x_sweep(g, carry):
        def put(i, values):
            block, rows = turned_rows(0, i, g)
            for f in range(FIELDS):
                change[f, block, rows, :] = change[f, block, rows, :] + values[f]

        plane_sweep(0, g, put)
        return carry

    lax.fori_loop(0, 4, x_sweep, 0)
    rim_copy = pltpu.make_async_copy(rim, rim_out, out_sems.at[FIELDS])
    rim_copy.start()
    copies = []
    for f in range(FIELDS):
        add_turned(change, partial, f, partial.at[f])
        copies.append(pltpu.make_async_copy(partial.at[f], out.at[f], out_sems.at[f]))
        copies[f].start()
    for copy in copies + [rim_copy]:
        copy.wait()


def add_turned(change, partial, f, result):
    back = (0.5 * DT_DX) * jnp.transpose(flat(change, f))
    for k in range(SLOTS):
        for c in range(LAYERS):
            n = (k * LAYERS + c) * 8
            for b in range(8):
                rows = pl.ds(8 * b, 8)
                result[k, c, rows, :] = (
                    partial[f, k, c, rows, :] - back[n : n + 8, 128 * b : 128 * (b + 1)]
                )


def inner(place, links, patches, z_below, z_above):
    return pl.pallas_call(
        inner_kernel,
        out_shape=[
            pltpu.HBM(PATCH_SHAPE, F32),
            pltpu.HBM(RIM_SHAPE, F32),
            jax.ShapeDtypeStruct((3 * LINKS,), jnp.int32),
        ],
        in_specs=[SMEM, SMEM, HBM, VMEM, VMEM],
        out_specs=[HBM, HBM, SMEM],
        scratch_shapes=[
            pltpu.VMEM(TURNED_SHAPE, F32),
            pltpu.VMEM(PATCH_SHAPE, F32),
            pltpu.VMEM(TURNED_SHAPE, F32),
            pltpu.VMEM(PATCH_SHAPE, F32),
            pltpu.VMEM(RIM_SHAPE, F32),
            pltpu.SemaphoreType.DMA((SLOTS,)),
            pltpu.SemaphoreType.DMA((FIELDS + 1,)),
        ],
        compiler_params=pltpu.CompilerParams(vmem_limit_bytes=24 * MIB),
        cost_estimate=LONG,
        name="inner",
    )(place, links, held(patches), z_below, z_above)


def outer_kernel(place, table, rim_in, arrived, own_items, partial_in, out, *scratch):
    rim, items, ghosts, change, partial, result, item_sems, sems, out_sems = scratch
    me = place[0]
    for i in range(LINKS):
        owner, rank, source = table[i], table[LINKS + i], table[2 * LINKS + i]

        @pl.when(owner != me)
        def _(i=i, owner=owner, rank=rank):
            pltpu.make_async_copy(arrived.at[owner, rank], items.at[i], item_sems.at[i]).start()

        @pl.when(owner == me)
        def _(i=i, source=source):
            pltpu.make_async_copy(own_items.at[source], items.at[i], item_sems.at[i]).start()

    loads = [
        pltpu.make_async_copy(rim_in, rim, sems.at[0]),
        pltpu.make_async_copy(partial_in, partial, sems.at[1]),
    ]
    for load in loads:
        load.start()
    change[...] = jnp.zeros(TURNED_SHAPE, F32)
    for i in range(LINKS):
        pltpu.make_async_copy(own_items.at[i], items.at[i], item_sems.at[i]).wait()
    for side in range(4):
        blocks = [items[k * 4 + side] for k in range(SLOTS)]
        for g, block in enumerate(block_transpose(blocks)):
            ghosts[side, g] = block
    loads[0].wait()

    def border(g, carry):
        for direction in (1, 0):

            def get(i):
                if 0 <= i < EDGE:
                    end, at = (0, i) if i < RIM else (1, i - EDGE + RIM)
                    return [rim[direction, end, at, f, g] for f in range(FIELDS)]
                side, layer = (0, i + GHOST) if i < 0 else (1, i - EDGE)
                rows = [pl.ds((f * GHOST + layer) * 8, 8) for f in range(FIELDS)]
                return primitives([ghosts[2 * direction + side, g, at, :] for at in rows])

            def put(i, values):
                block, rows = turned_rows(direction, i, g)
                for f in range(FIELDS):
                    change[f, block, rows, :] = change[f, block, rows, :] + values[f]

            sweep(get, put, direction, -1, 1)
            sweep(get, put, direction, EDGE - 3, EDGE - 1)
        return carry

    lax.fori_loop(0, 4, border, 0)
    loads[1].wait()
    copies = []
    for f in range(FIELDS):
        add_turned(change, partial, f, result.at[f])
        copies.append(pltpu.make_async_copy(result.at[f], out.at[:, f], out_sems.at[f]))
        copies[f].start()
    for copy in copies:
        copy.wait()


def outer(place, table, rim, arrived, own_items, partial):
    return pl.pallas_call(
        outer_kernel,
        out_shape=jax.ShapeDtypeStruct((SLOTS, FIELDS, LAYERS, 64, 128), F32),
        in_specs=[SMEM, SMEM] + [HBM] * 4,
        out_specs=HBM,
        scratch_shapes=[
            pltpu.VMEM(RIM_SHAPE, F32),
            pltpu.VMEM((LINKS, ITEM_ROWS, 128), F32),
            pltpu.VMEM((4, 4, ITEM_ROWS, 128), F32),
            pltpu.VMEM(TURNED_SHAPE, F32),
            pltpu.VMEM(PATCH_SHAPE, F32),
            pltpu.VMEM(PATCH_SHAPE, F32),
            pltpu.SemaphoreType.DMA((LINKS,)),
            pltpu.SemaphoreType.DMA((2,)),
            pltpu.SemaphoreType.DMA((FIELDS,)),
        ],
        compiler_params=pltpu.CompilerParams(vmem_limit_bytes=24 * MIB),
        name="outer",
    )(place, table, held(rim), held(arrived), held(own_items), held(partial))


def local(cells, moves, neighbours):
    tiled = cells.reshape(SLOTS, FIELDS, LAYERS, 8, 8, 128).transpose(0, 1, 2, 4, 3, 5)
    tiled = tiled.reshape(SLOTS, FIELDS * LAYERS, 64, 128)
    plan = moves[lax.axis_index(("gx", "gy", "gz"))].reshape(-1)
    place = lax.axis_index(("gx", "gy")).reshape(1)
    links = neighbours.reshape(-1)

    got, after = migrate(plan, tiled)
    made = ()
    for fields in GROUPS:
        received = [got[r, c] for c in chunks_of(fields) for r in range(3)]
        made = faces(fields, plan, place, links, tiled, received, after, made)
    patches, send, own_items, z_first, z_last = made

    arrived = lax.all_to_all(send, ("gx", "gy"), 0, 0, tiled=True)
    layers = lax.axis_size("gz")
    up = [(i, (i + 1) % layers) for i in range(layers)]
    down = [(j, i) for i, j in up]
    z_below = lax.ppermute(z_last, "gz", up)
    z_above = lax.ppermute(z_first, "gz", down)
    partial, rim, table = inner(place, links, patches, z_below, z_above)
    result = outer(place, table, rim, arrived, own_items, partial)
    result = result.reshape(SLOTS, FIELDS, LAYERS, 8, 8, 128).transpose(0, 1, 2, 4, 3, 5)
    return result.reshape(cells.shape)


def solution(mesh):
    return jax.shard_map(
        local,
        mesh=mesh,
        in_specs=(P(("gx", "gy", "gz"), None, None, None), P(), P()),
        out_specs=P(("gx", "gy", "gz"), None, None, None),
        check_vma=False,
    )
```

```python
import functools

import jax
import jax.numpy as jnp
from jax import lax
from jax.experimental import pallas as pl
from jax.experimental.pallas import tpu as pltpu
from jax.sharding import PartitionSpec as P

GAMMA = 5.0 / 3.0
DT_DX = 0.02
EDGE = 32
GHOST = 3
SLOTS = 4
LAYERS = 4
FIELDS = 5
PLANE = 16
LINKS = 16
GROUPS = ((0, 1, 2), (3, 4))
ITEM_ROWS = FIELDS * GHOST * 8
PATCH_SHAPE = (FIELDS, SLOTS, LAYERS, 64, 128)
PITCH = EDGE + 8
TURNED_SHAPE = (FIELDS, 4, 8 * PITCH, 128)
RIM = GHOST + 2
RIM_SHAPE = (2, 2, RIM, FIELDS, 4, 8, 128)
MIB = 1024 * 1024

F32 = jnp.float32
ANY = pl.BlockSpec(memory_space=pl.ANY)
HBM = pl.BlockSpec(memory_space=pltpu.HBM)
SMEM = pl.BlockSpec(memory_space=pltpu.SMEM)
VMEM = pl.BlockSpec(memory_space=pltpu.VMEM)
LONG = pl.CostEstimate(flops=10**12, bytes_accessed=10**10, transcendentals=10**10)
CHUNKS = (4, 4, 4, 4, 4)
STARTS = tuple(sum(CHUNKS[:c]) for c in range(len(CHUNKS)))


def held(x):
    return pltpu.with_memory_space_constraint(x, pltpu.HBM)


def start_copies(plan, slot, rounds, cells, jobs):
    taken = jnp.bool_(False)
    for r in reversed(range(rounds)):
        for j in range(2):
            hit = jnp.logical_and(plan[2 * r + j] == slot, jnp.logical_not(taken))

            @pl.when(hit)
            def _(r=r, j=j):
                for _, received, first, count, target, sem in jobs:
                    source = received[r].at[j, pl.ds(first, count)]
                    pltpu.make_async_copy(source, target, sem).start()

            taken = jnp.logical_or(taken, hit)

    @pl.when(jnp.logical_not(taken))
    def _():
        for chunk, _, first, count, target, sem in jobs:
            source = cells.at[slot, pl.ds(STARTS[chunk] + first, count)]
            pltpu.make_async_copy(source, target, sem).start()


def wait_copy(cells, count, target, sem):
    pltpu.make_async_copy(cells.at[0, pl.ds(0, count)], target, sem).wait()


def pack_kernel(sends, taken, plan, cells, *refs):
    received, refs = refs[:taken], refs[-len(sends) - 1 :]
    outs, sems = refs[:-1], refs[-1]
    at = 0
    for n, (r, c) in enumerate(sends):
        got = received[at : at + r]
        at += r
        for j in range(2):
            job = (c, got, 0, CHUNKS[c], outs[n].at[j], sems.at[n, j])
            start_copies(plan, plan[2 * r + j], r, cells, [job])
    for n, (r, c) in enumerate(sends):
        for j in range(2):
            wait_copy(cells, CHUNKS[c], outs[n].at[j], sems.at[n, j])


def pack(sends, plan, cells, received, after):
    return pl.pallas_call(
        functools.partial(pack_kernel, sends, len(received)),
        out_shape=[jax.ShapeDtypeStruct((2, CHUNKS[c], 64, 128), F32) for _, c in sends],
        in_specs=[SMEM, HBM] + [ANY] * (len(received) + len(after)),
        out_specs=[VMEM] * len(sends),
        scratch_shapes=[pltpu.SemaphoreType.DMA((len(sends), 2))],
        compiler_params=pltpu.CompilerParams(vmem_limit_bytes=4 * MIB),
        name="pack",
    )(plan, held(cells), *received, *after)


def swapped(block, axis):
    count = lax.axis_size(axis)
    return lax.ppermute(block, axis, [(i, i ^ (count // 2)) for i in range(count)])


WAVES = (
    ([(0, 0)], []),
    ([(0, 1), (0, 2)], []),
    ([(0, 3), (0, 4)], []),
    ([(1, 0)], []),
    ([(1, 1)], []),
    ([(1, 2), (2, 0)], []),
    ([(1, 3), (2, 1)], []),
    ([(1, 4), (2, 2)], [(2, 0)]),
    ([(2, 3)], [(2, 1)]),
    ([(2, 4)], [(2, 1)]),
)


def migrate(plan, cells):
    got, last = {}, []
    for sends, awaited in WAVES:
        received = [got[i, c] for r, c in sends for i in range(r)]
        after = list(last[-1:]) + [got[at] for at in awaited]
        last = pack(sends, plan, cells, received, after)
        for (r, c), block in zip(sends, last):
            got[r, c] = swapped(block, ("gx", "gy", "gz")[r])
    return got, last[-1]


def primitives(u):
    inv = 1.0 / u[0]
    v = [u[i] * inv for i in (1, 2, 3)]
    kinetic = u[1] * v[0] + u[2] * v[1] + u[3] * v[2]
    return [u[0]] + v + [(GAMMA - 1.0) * (u[4] - 0.5 * kinetic)]


def block_transpose(b):
    lane = lax.broadcasted_iota(jnp.int32, b[0].shape, 1)
    low = lane < 64
    even = (lane & 32) == 0

    def rolled(x, shift):
        return pltpu.roll(x, shift, 1)

    a0 = jnp.where(low, b[0], rolled(b[2], 64))
    a2 = jnp.where(low, rolled(b[0], 64), b[2])
    a1 = jnp.where(low, b[1], rolled(b[3], 64))
    a3 = jnp.where(low, rolled(b[1], 64), b[3])
    return [
        jnp.where(even, a0, rolled(a1, 32)),
        jnp.where(even, rolled(a0, 96), a1),
        jnp.where(even, a2, rolled(a3, 32)),
        jnp.where(even, rolled(a2, 96), a3),
    ]


def y_rows(i, g):
    return pl.ds(pl.multiple_of((i % 8) * PITCH + 8 * g, 8), 8)


def turned_rows(direction, i, g):
    if direction == 0:
        return g, pl.ds(i, 8, stride=PITCH)
    return i // 8, y_rows(i, g)


def flat(turned, f):
    rows = [turned[f, g, pl.ds(y * PITCH, EDGE), :] for g in range(4) for y in range(8)]
    return jnp.concatenate(rows, axis=0)


def turn(patches, turned, n):
    columns = [
        jnp.concatenate(
            [patches[n, k, c, pl.ds(8 * b, 8), :] for k in range(SLOTS) for c in range(LAYERS)],
            axis=0,
        )
        for b in range(8)
    ]
    rows = jnp.transpose(jnp.concatenate(columns, axis=1))
    for y in range(EDGE):
        turned[n, y // 8, pl.ds(y % 8 * PITCH, EDGE), :] = rows[y * EDGE : (y + 1) * EDGE]


def pieces(f):
    out = []
    for c, start in enumerate(STARTS):
        low, high = max(start, f * LAYERS), min(start + CHUNKS[c], (f + 1) * LAYERS)
        if low < high:
            out.append((c, low - start, high - low, low - f * LAYERS))
    return out


def chunks_of(fields):
    return sorted({c for f in fields for c, _, _, _ in pieces(f)})


def faces_kernel(fields, plan, place, links, cells, *refs):
    count, first, last = len(fields), fields[0], fields[0] > 0
    chunks = chunks_of(fields)
    received = refs[: 3 * len(chunks)]
    refs = refs[3 * len(chunks) + 1 + 3 * last :]
    patches_out, send, own_items = refs[:3]
    patches, turned, items, sems, item_sems, out_sem = refs[-6:]
    parts = []
    for k in range(SLOTS):
        jobs = []
        for n, f in enumerate(fields):
            for p, (c, start, size, layer) in enumerate(pieces(f)):
                got = received[3 * chunks.index(c) : 3 * chunks.index(c) + 3]
                target, sem = patches.at[n, k, pl.ds(layer, size)], sems.at[n, k, p]
                jobs.append((c, got, start, size, target, sem))
                parts.append((n, size, target, sem))
        start_copies(plan, k, 3, cells, jobs)
    loads = []
    if last:
        z_first, z_last, ends, end_sems = refs[3:7]
        for end, c in ((0, 0), (1, LAYERS - 1)):
            source = patches_out.at[pl.ds(0, first), :, c]
            loads.append(pltpu.make_async_copy(source, ends.at[end], end_sems.at[end]))
    for load in loads:
        load.start()

    whole = [
        pltpu.make_async_copy(patches.at[n], patches_out.at[f], out_sem.at[n])
        for n, f in enumerate(fields)
    ]
    for n, f in enumerate(fields):
        for at, size, target, sem in parts:
            if at == n:
                wait_copy(cells, size, target, sem)
        whole[n].start()
        turn(patches, turned, n)

    me = place[0]
    owners = [links[me * LINKS + i] // SLOTS for i in range(LINKS)]
    rows = pl.ds(first * GHOST * 8, count * GHOST * 8)
    for side in range(4):
        start = EDGE - GHOST if side % 2 else 0
        blocks = []
        for g in range(4):
            tiles = []
            for n in range(count):
                for layer in range(start, start + GHOST):
                    block, where = turned_rows(side // 2, layer, g)
                    tiles.append(turned[n, block, where, :])
            blocks.append(jnp.concatenate(tiles, axis=0))
        for k, block in enumerate(block_transpose(blocks)):
            items[k * 4 + side] = block
        for i in range(side, LINKS, 4):
            rank = jnp.int32(0)
            for j in range(i):
                rank = rank + (owners[j] == owners[i]).astype(jnp.int32)
            rank = jnp.minimum(rank, 1)

            @pl.when(owners[i] != me)
            def _(i=i, rank=rank):
                target = send.at[owners[i], rank, rows]
                pltpu.make_async_copy(items.at[i], target, item_sems.at[i]).start()

            @pl.when(owners[i] == me)
            def _(i=i):
                target = own_items.at[i, rows]
                pltpu.make_async_copy(items.at[i], target, item_sems.at[i]).start()

    for load in loads:
        load.wait()
    if last:
        for f in range(FIELDS):
            for k in range(SLOTS):
                if f < first:
                    head, tail = ends.at[0, f, k], ends.at[1, f, k]
                else:
                    head, tail = patches.at[f - first, k, 0], patches.at[f - first, k, LAYERS - 1]
                for layer in range(GHOST):
                    z_first[k, f, layer] = head[pl.ds(layer, 8, stride=8), :]
                    z_last[k, f, layer] = tail[pl.ds(8 - GHOST + layer, 8, stride=8), :]

    for i in range(LINKS):
        pltpu.make_async_copy(items.at[i], own_items.at[i, rows], item_sems.at[i]).wait()
    for copy in whole:
        copy.wait()


def faces(fields, plan, place, links, cells, received, after, carried):
    count, first, last = len(fields), fields[0], fields[0] > 0
    held_chunks = 3 * len(chunks_of(fields))
    z_shape = jax.ShapeDtypeStruct((SLOTS, FIELDS, GHOST, 8, 128), F32)
    scratch = [
        pltpu.VMEM((count,) + PATCH_SHAPE[1:], F32),
        pltpu.VMEM((count,) + TURNED_SHAPE[1:], F32),
        pltpu.VMEM((LINKS, count * GHOST * 8, 128), F32),
        pltpu.SemaphoreType.DMA((count, SLOTS, 2)),
        pltpu.SemaphoreType.DMA((LINKS,)),
        pltpu.SemaphoreType.DMA((count,)),
    ]
    if last:
        scratch = [
            pltpu.VMEM((2, first, SLOTS, 64, 128), F32),
            pltpu.SemaphoreType.DMA((2,)),
        ] + scratch
    inputs = [held(cells)] + list(received) + [after] + [held(x) for x in carried]
    return pl.pallas_call(
        functools.partial(faces_kernel, fields),
        out_shape=[
            pltpu.HBM(PATCH_SHAPE, F32),
            pltpu.HBM((PLANE, 2, ITEM_ROWS, 128), F32),
            pltpu.HBM((LINKS, ITEM_ROWS, 128), F32),
        ]
        + [z_shape] * (2 * last),
        in_specs=[SMEM] * 3 + [HBM] + [ANY] * (held_chunks + 1) + [HBM] * len(carried),
        out_specs=[HBM] * 3 + [VMEM] * (2 * last),
        scratch_shapes=scratch,
        input_output_aliases={held_chunks + 5 + i: i for i in range(len(carried))},
        compiler_params=pltpu.CompilerParams(vmem_limit_bytes=16 * MIB),
        cost_estimate=LONG if last else None,
        name="faces",
    )(plan, place, links, *inputs)


def clamped(x, y):
    return jnp.minimum(jnp.maximum(x, jnp.minimum(y, 0.0)), jnp.maximum(y, 0.0))


def euler_terms(w, normal):
    density, velocity, pressure = w[0], w[1:4], w[4]
    speed = velocity[normal]
    momentum = [density * v for v in velocity]
    kinetic = momentum[0] * velocity[0] + momentum[1] * velocity[1] + momentum[2] * velocity[2]
    energy = 1.5 * pressure + 0.5 * kinetic
    flux = [momentum[normal]]
    for i in range(3):
        term = momentum[i] * speed
        flux.append(term + pressure if i == normal else term)
    flux.append((energy + pressure) * speed)
    stiff = GAMMA * pressure
    signal = jnp.abs(speed) + stiff * lax.rsqrt(stiff * density)
    return [density] + momentum + [energy], flux, signal


def sweep(get, put, normal, first, last):
    w, d, a, b = {}, {}, {}, {}
    prev, left = None, None
    start = first - 2
    for i in range(start, last + 4):
        w[i] = get(i)
        if i == start:
            continue
        d[i - 1] = [hi - lo for hi, lo in zip(w[i], w[i - 1])]
        m = i - 2
        if m <= start:
            continue
        a[m] = [
            clamped(0.5 * mid - (1.0 / 12.0) * (up - down), mid)
            for down, mid, up in zip(d[m - 1], d[m], d[m + 1])
        ]
        b[m + 1] = [mid - part for mid, part in zip(d[m], a[m])]
        if m < first:
            continue
        if m > first:
            lower = [v - clamped(y, 2.0 * x) for v, x, y in zip(w[m], a[m], b[m])]
            right = euler_terms(lower, normal)
            fastest = jnp.maximum(left[2], right[2])
            flux = [
                gl + gr - fastest * (ur - ul)
                for gl, gr, ul, ur in zip(left[1], right[1], left[0], right[0])
            ]
            if prev is not None:
                put(m - 1, [new - old for new, old in zip(flux, prev)])
            elif m > 0:
                put(m - 1, flux)
            prev = flux
        if m <= last:
            upper = [v + clamped(x, 2.0 * y) for v, x, y in zip(w[m], a[m], b[m])]
            left = euler_terms(upper, normal)
    if last + 1 < EDGE:
        put(last + 1, [-v for v in prev])


def inner_kernel(place, links, patches_in, z_below, z_above, out, rim_out, table, *scratch):
    turned, patches, change, partial, rim, sems, out_sems = scratch
    loads = [
        pltpu.make_async_copy(patches_in.at[:, k], patches.at[:, k], sems.at[k])
        for k in range(SLOTS)
    ]
    for load in loads:
        load.start()
    me = place[0]
    for i in range(LINKS):
        entry = links[me * LINKS + i]
        owner = entry // SLOTS
        source = (entry % SLOTS) * 4 + (i % 4 ^ 1)
        rank = jnp.int32(0)
        for j in range(LINKS - 1):
            same = jnp.logical_and(links[owner * LINKS + j] // SLOTS == me, j < source)
            rank = rank + same.astype(jnp.int32)
        table[i] = owner
        table[LINKS + i] = jnp.minimum(rank, 1)
        table[2 * LINKS + i] = source
    for load in loads:
        load.wait()
    for f in range(FIELDS):
        turn(patches, turned, f)

    def z_sweep(k, carry):
        def get(i):
            if i < 0:
                u = [z_below[k, f, i + GHOST] for f in range(FIELDS)]
            elif i >= EDGE:
                u = [z_above[k, f, i - EDGE] for f in range(FIELDS)]
            else:
                rows = pl.ds(i % 8, 8, stride=8)
                u = [patches[f, k, i // 8, rows, :] for f in range(FIELDS)]
            return primitives(u)

        def put(i, values):
            rows = pl.ds(i % 8, 8, stride=8)
            for f in range(FIELDS):
                partial[f, k, i // 8, rows, :] = (
                    patches[f, k, i // 8, rows, :] - (0.5 * DT_DX) * values[f]
                )

        sweep(get, put, 2, -1, EDGE - 1)
        return carry

    lax.fori_loop(0, SLOTS, z_sweep, 0)

    def plane_sweep(direction, g, put):
        def get(i):
            block, rows = turned_rows(direction, i, g)
            w = primitives([turned[f, block, rows, :] for f in range(FIELDS)])
            end, at = (0, i) if i < RIM else (1, i - EDGE + RIM)
            if 0 <= at < RIM:
                for f in range(FIELDS):
                    rim[direction, end, at, f, g] = w[f]
            return w

        sweep(get, put, direction, 2, EDGE - 4)

    def y_sweep(g, carry):
        def put(i, values):
            block, rows = turned_rows(1, i, g)
            for f in range(FIELDS):
                change[f, block, rows, :] = values[f]

        for i in (0, 1, EDGE - 2, EDGE - 1):
            put(i, [jnp.zeros((8, 128), F32)] * FIELDS)
        plane_sweep(1, g, put)
        return carry

    lax.fori_loop(0, 4, y_sweep, 0)

    def x_sweep(g, carry):
        def put(i, values):
            block, rows = turned_rows(0, i, g)
            for f in range(FIELDS):
                change[f, block, rows, :] = change[f, block, rows, :] + values[f]

        plane_sweep(0, g, put)
        return carry

    lax.fori_loop(0, 4, x_sweep, 0)
    rim_copy = pltpu.make_async_copy(rim, rim_out, out_sems.at[FIELDS])
    rim_copy.start()
    copies = []
    for f in range(FIELDS):
        add_turned(change, partial, f, partial.at[f])
        copies.append(pltpu.make_async_copy(partial.at[f], out.at[f], out_sems.at[f]))
        copies[f].start()
    for copy in copies + [rim_copy]:
        copy.wait()


def add_turned(change, partial, f, result):
    back = (0.5 * DT_DX) * jnp.transpose(flat(change, f))
    for k in range(SLOTS):
        for c in range(LAYERS):
            n = (k * LAYERS + c) * 8
            for b in range(8):
                rows = pl.ds(8 * b, 8)
                result[k, c, rows, :] = (
                    partial[f, k, c, rows, :] - back[n : n + 8, 128 * b : 128 * (b + 1)]
                )


def inner(place, links, patches, z_below, z_above):
    return pl.pallas_call(
        inner_kernel,
        out_shape=[
            pltpu.HBM(PATCH_SHAPE, F32),
            pltpu.HBM(RIM_SHAPE, F32),
            jax.ShapeDtypeStruct((3 * LINKS,), jnp.int32),
        ],
        in_specs=[SMEM, SMEM, HBM, VMEM, VMEM],
        out_specs=[HBM, HBM, SMEM],
        scratch_shapes=[
            pltpu.VMEM(TURNED_SHAPE, F32),
            pltpu.VMEM(PATCH_SHAPE, F32),
            pltpu.VMEM(TURNED_SHAPE, F32),
            pltpu.VMEM(PATCH_SHAPE, F32),
            pltpu.VMEM(RIM_SHAPE, F32),
            pltpu.SemaphoreType.DMA((SLOTS,)),
            pltpu.SemaphoreType.DMA((FIELDS + 1,)),
        ],
        compiler_params=pltpu.CompilerParams(vmem_limit_bytes=24 * MIB),
        cost_estimate=LONG,
        name="inner",
    )(place, links, held(patches), z_below, z_above)


def outer_kernel(place, table, rim_in, arrived, own_items, partial_in, out, *scratch):
    rim, items, ghosts, change, partial, result, item_sems, sems, out_sems = scratch
    me = place[0]
    for i in range(LINKS):
        owner, rank, source = table[i], table[LINKS + i], table[2 * LINKS + i]

        @pl.when(owner != me)
        def _(i=i, owner=owner, rank=rank):
            pltpu.make_async_copy(arrived.at[owner, rank], items.at[i], item_sems.at[i]).start()

        @pl.when(owner == me)
        def _(i=i, source=source):
            pltpu.make_async_copy(own_items.at[source], items.at[i], item_sems.at[i]).start()

    loads = [
        pltpu.make_async_copy(rim_in, rim, sems.at[0]),
        pltpu.make_async_copy(partial_in, partial, sems.at[1]),
    ]
    for load in loads:
        load.start()
    change[...] = jnp.zeros(TURNED_SHAPE, F32)
    for i in range(LINKS):
        pltpu.make_async_copy(own_items.at[i], items.at[i], item_sems.at[i]).wait()
    for side in range(4):
        blocks = [items[k * 4 + side] for k in range(SLOTS)]
        for g, block in enumerate(block_transpose(blocks)):
            ghosts[side, g] = block
    loads[0].wait()

    def border(g, carry):
        for direction in (1, 0):

            def get(i):
                if 0 <= i < EDGE:
                    end, at = (0, i) if i < RIM else (1, i - EDGE + RIM)
                    return [rim[direction, end, at, f, g] for f in range(FIELDS)]
                side, layer = (0, i + GHOST) if i < 0 else (1, i - EDGE)
                rows = [pl.ds((f * GHOST + layer) * 8, 8) for f in range(FIELDS)]
                return primitives([ghosts[2 * direction + side, g, at, :] for at in rows])

            def put(i, values):
                block, rows = turned_rows(direction, i, g)
                for f in range(FIELDS):
                    change[f, block, rows, :] = change[f, block, rows, :] + values[f]

            sweep(get, put, direction, -1, 1)
            sweep(get, put, direction, EDGE - 3, EDGE - 1)
        return carry

    lax.fori_loop(0, 4, border, 0)
    loads[1].wait()
    copies = []
    for f in range(FIELDS):
        add_turned(change, partial, f, result.at[f])
        copies.append(pltpu.make_async_copy(result.at[f], out.at[:, f], out_sems.at[f]))
        copies[f].start()
    for copy in copies:
        copy.wait()


def outer(place, table, rim, arrived, own_items, partial):
    return pl.pallas_call(
        outer_kernel,
        out_shape=jax.ShapeDtypeStruct((SLOTS, FIELDS, LAYERS, 64, 128), F32),
        in_specs=[SMEM, SMEM] + [HBM] * 4,
        out_specs=HBM,
        scratch_shapes=[
            pltpu.VMEM(RIM_SHAPE, F32),
            pltpu.VMEM((LINKS, ITEM_ROWS, 128), F32),
            pltpu.VMEM((4, 4, ITEM_ROWS, 128), F32),
            pltpu.VMEM(TURNED_SHAPE, F32),
            pltpu.VMEM(PATCH_SHAPE, F32),
            pltpu.VMEM(PATCH_SHAPE, F32),
            pltpu.SemaphoreType.DMA((LINKS,)),
            pltpu.SemaphoreType.DMA((2,)),
            pltpu.SemaphoreType.DMA((FIELDS,)),
        ],
        compiler_params=pltpu.CompilerParams(vmem_limit_bytes=24 * MIB),
        name="outer",
    )(place, table, held(rim), held(arrived), held(own_items), held(partial))


def local(cells, moves, neighbours):
    tiled = cells.reshape(SLOTS, FIELDS, LAYERS, 8, 8, 128).transpose(0, 1, 2, 4, 3, 5)
    tiled = tiled.reshape(SLOTS, FIELDS * LAYERS, 64, 128)
    plan = moves[lax.axis_index(("gx", "gy", "gz"))].reshape(-1)
    place = lax.axis_index(("gx", "gy")).reshape(1)
    links = neighbours.reshape(-1)

    got, after = migrate(plan, tiled)
    made = ()
    for fields in GROUPS:
        received = [got[r, c] for c in chunks_of(fields) for r in range(3)]
        made = faces(fields, plan, place, links, tiled, received, after, made)
    patches, send, own_items, z_first, z_last = made

    arrived = lax.all_to_all(send, ("gx", "gy"), 0, 0, tiled=True)
    layers = lax.axis_size("gz")
    up = [(i, (i + 1) % layers) for i in range(layers)]
    down = [(j, i) for i, j in up]
    z_below = lax.ppermute(z_last, "gz", up)
    z_above = lax.ppermute(z_first, "gz", down)
    partial, rim, table = inner(place, links, patches, z_below, z_above)
    result = outer(place, table, rim, arrived, own_items, partial)
    result = result.reshape(SLOTS, FIELDS, LAYERS, 8, 8, 128).transpose(0, 1, 2, 4, 3, 5)
    return result.reshape(cells.shape)


def solution(mesh):
    return jax.shard_map(
        local,
        mesh=mesh,
        in_specs=(P(("gx", "gy", "gz"), None, None, None), P(), P()),
        out_specs=P(("gx", "gy", "gz"), None, None, None),
        check_vma=False,
    )
```

```python
import functools

import jax
import jax.numpy as jnp
from jax import lax
from jax.experimental import pallas as pl
from jax.experimental.pallas import tpu as pltpu
from jax.sharding import PartitionSpec as P

GAMMA = 5.0 / 3.0
DT_DX = 0.02
EDGE = 32
GHOST = 3
SLOTS = 4
LAYERS = 4
FIELDS = 5
PLANE = 16
LINKS = 16
GROUPS = ((0, 1, 2), (3, 4))
ITEM_ROWS = FIELDS * GHOST * 8
PATCH_SHAPE = (FIELDS, SLOTS, LAYERS, 64, 128)
PITCH = EDGE + 8
TURNED_SHAPE = (FIELDS, 4, 8 * PITCH, 128)
RIM = GHOST + 2
RIM_SHAPE = (2, 2, RIM, FIELDS, 4, 8, 128)
MIB = 1024 * 1024

F32 = jnp.float32
ANY = pl.BlockSpec(memory_space=pl.ANY)
HBM = pl.BlockSpec(memory_space=pltpu.HBM)
SMEM = pl.BlockSpec(memory_space=pltpu.SMEM)
VMEM = pl.BlockSpec(memory_space=pltpu.VMEM)
LONG = pl.CostEstimate(flops=10**12, bytes_accessed=10**10, transcendentals=10**10)
CHUNKS = (4, 4, 4, 4, 4)
STARTS = tuple(sum(CHUNKS[:c]) for c in range(len(CHUNKS)))


def held(x):
    return pltpu.with_memory_space_constraint(x, pltpu.HBM)


def start_copies(plan, slot, rounds, cells, jobs):
    taken = jnp.bool_(False)
    for r in reversed(range(rounds)):
        for j in range(2):
            hit = jnp.logical_and(plan[2 * r + j] == slot, jnp.logical_not(taken))

            @pl.when(hit)
            def _(r=r, j=j):
                for _, received, first, count, target, sem in jobs:
                    source = received[r].at[j, pl.ds(first, count)]
                    pltpu.make_async_copy(source, target, sem).start()

            taken = jnp.logical_or(taken, hit)

    @pl.when(jnp.logical_not(taken))
    def _():
        for chunk, _, first, count, target, sem in jobs:
            source = cells.at[slot, pl.ds(STARTS[chunk] + first, count)]
            pltpu.make_async_copy(source, target, sem).start()


def wait_copy(cells, count, target, sem):
    pltpu.make_async_copy(cells.at[0, pl.ds(0, count)], target, sem).wait()


def pack_kernel(sends, taken, plan, cells, *refs):
    received, refs = refs[:taken], refs[-len(sends) - 1 :]
    outs, sems = refs[:-1], refs[-1]
    at = 0
    for n, (r, c) in enumerate(sends):
        got = received[at : at + r]
        at += r
        for j in range(2):
            job = (c, got, 0, CHUNKS[c], outs[n].at[j], sems.at[n, j])
            start_copies(plan, plan[2 * r + j], r, cells, [job])
    for n, (r, c) in enumerate(sends):
        for j in range(2):
            wait_copy(cells, CHUNKS[c], outs[n].at[j], sems.at[n, j])


def pack(sends, plan, cells, received, after):
    return pl.pallas_call(
        functools.partial(pack_kernel, sends, len(received)),
        out_shape=[jax.ShapeDtypeStruct((2, CHUNKS[c], 64, 128), F32) for _, c in sends],
        in_specs=[SMEM, HBM] + [ANY] * (len(received) + len(after)),
        out_specs=[VMEM] * len(sends),
        scratch_shapes=[pltpu.SemaphoreType.DMA((len(sends), 2))],
        compiler_params=pltpu.CompilerParams(vmem_limit_bytes=4 * MIB),
        name="pack",
    )(plan, held(cells), *received, *after)


def swapped(block, axis):
    count = lax.axis_size(axis)
    return lax.ppermute(block, axis, [(i, i ^ (count // 2)) for i in range(count)])


WAVES = (
    ([(0, 0)], []),
    ([(0, 1), (0, 2)], []),
    ([(0, 3), (0, 4)], []),
    ([(1, 0)], []),
    ([(1, 1)], []),
    ([(1, 2), (2, 0)], []),
    ([(1, 3), (2, 1)], []),
    ([(1, 4), (2, 2)], []),
    ([(2, 3)], [(2, 0)]),
    ([(2, 4)], [(2, 1)]),
)


def migrate(plan, cells):
    got, last = {}, []
    for sends, awaited in WAVES:
        received = [got[i, c] for r, c in sends for i in range(r)]
        after = list(last[-1:]) + [got[at] for at in awaited]
        last = pack(sends, plan, cells, received, after)
        for (r, c), block in zip(sends, last):
            got[r, c] = swapped(block, ("gx", "gy", "gz")[r])
    return got, last[-1]


def primitives(u):
    inv = 1.0 / u[0]
    v = [u[i] * inv for i in (1, 2, 3)]
    kinetic = u[1] * v[0] + u[2] * v[1] + u[3] * v[2]
    return [u[0]] + v + [(GAMMA - 1.0) * (u[4] - 0.5 * kinetic)]


def block_transpose(b):
    lane = lax.broadcasted_iota(jnp.int32, b[0].shape, 1)
    low = lane < 64
    even = (lane & 32) == 0

    def rolled(x, shift):
        return pltpu.roll(x, shift, 1)

    a0 = jnp.where(low, b[0], rolled(b[2], 64))
    a2 = jnp.where(low, rolled(b[0], 64), b[2])
    a1 = jnp.where(low, b[1], rolled(b[3], 64))
    a3 = jnp.where(low, rolled(b[1], 64), b[3])
    return [
        jnp.where(even, a0, rolled(a1, 32)),
        jnp.where(even, rolled(a0, 96), a1),
        jnp.where(even, a2, rolled(a3, 32)),
        jnp.where(even, rolled(a2, 96), a3),
    ]


def y_rows(i, g):
    return pl.ds(pl.multiple_of((i % 8) * PITCH + 8 * g, 8), 8)


def turned_rows(direction, i, g):
    if direction == 0:
        return g, pl.ds(i, 8, stride=PITCH)
    return i // 8, y_rows(i, g)


def flat(turned, f):
    rows = [turned[f, g, pl.ds(y * PITCH, EDGE), :] for g in range(4) for y in range(8)]
    return jnp.concatenate(rows, axis=0)


def turn(patches, turned, n):
    columns = [
        jnp.concatenate(
            [patches[n, k, c, pl.ds(8 * b, 8), :] for k in range(SLOTS) for c in range(LAYERS)],
            axis=0,
        )
        for b in range(8)
    ]
    rows = jnp.transpose(jnp.concatenate(columns, axis=1))
    for y in range(EDGE):
        turned[n, y // 8, pl.ds(y % 8 * PITCH, EDGE), :] = rows[y * EDGE : (y + 1) * EDGE]


def pieces(f):
    out = []
    for c, start in enumerate(STARTS):
        low, high = max(start, f * LAYERS), min(start + CHUNKS[c], (f + 1) * LAYERS)
        if low < high:
            out.append((c, low - start, high - low, low - f * LAYERS))
    return out


def chunks_of(fields):
    return sorted({c for f in fields for c, _, _, _ in pieces(f)})


def faces_kernel(fields, plan, place, links, cells, *refs):
    count, first, last = len(fields), fields[0], fields[0] > 0
    chunks = chunks_of(fields)
    received = refs[: 3 * len(chunks)]
    refs = refs[3 * len(chunks) + 1 + 3 * last :]
    patches_out, send, own_items = refs[:3]
    patches, turned, items, sems, item_sems, out_sem = refs[-6:]
    parts = []
    for k in range(SLOTS):
        jobs = []
        for n, f in enumerate(fields):
            for p, (c, start, size, layer) in enumerate(pieces(f)):
                got = received[3 * chunks.index(c) : 3 * chunks.index(c) + 3]
                target, sem = patches.at[n, k, pl.ds(layer, size)], sems.at[n, k, p]
                jobs.append((c, got, start, size, target, sem))
                parts.append((n, size, target, sem))
        start_copies(plan, k, 3, cells, jobs)
    loads = []
    if last:
        z_first, z_last, ends, end_sems = refs[3:7]
        for end, c in ((0, 0), (1, LAYERS - 1)):
            source = patches_out.at[pl.ds(0, first), :, c]
            loads.append(pltpu.make_async_copy(source, ends.at[end], end_sems.at[end]))
    for load in loads:
        load.start()

    whole = [
        pltpu.make_async_copy(patches.at[n], patches_out.at[f], out_sem.at[n])
        for n, f in enumerate(fields)
    ]
    for n, f in enumerate(fields):
        for at, size, target, sem in parts:
            if at == n:
                wait_copy(cells, size, target, sem)
        whole[n].start()
        turn(patches, turned, n)

    me = place[0]
    owners = [links[me * LINKS + i] // SLOTS for i in range(LINKS)]
    rows = pl.ds(first * GHOST * 8, count * GHOST * 8)
    for side in range(4):
        start = EDGE - GHOST if side % 2 else 0
        blocks = []
        for g in range(4):
            tiles = []
            for n in range(count):
                for layer in range(start, start + GHOST):
                    block, where = turned_rows(side // 2, layer, g)
                    tiles.append(turned[n, block, where, :])
            blocks.append(jnp.concatenate(tiles, axis=0))
        for k, block in enumerate(block_transpose(blocks)):
            items[k * 4 + side] = block
        for i in range(side, LINKS, 4):
            rank = jnp.int32(0)
            for j in range(i):
                rank = rank + (owners[j] == owners[i]).astype(jnp.int32)
            rank = jnp.minimum(rank, 1)

            @pl.when(owners[i] != me)
            def _(i=i, rank=rank):
                target = send.at[owners[i], rank, rows]
                pltpu.make_async_copy(items.at[i], target, item_sems.at[i]).start()

            @pl.when(owners[i] == me)
            def _(i=i):
                target = own_items.at[i, rows]
                pltpu.make_async_copy(items.at[i], target, item_sems.at[i]).start()

    for load in loads:
        load.wait()
    if last:
        for f in range(FIELDS):
            for k in range(SLOTS):
                if f < first:
                    head, tail = ends.at[0, f, k], ends.at[1, f, k]
                else:
                    head, tail = patches.at[f - first, k, 0], patches.at[f - first, k, LAYERS - 1]
                for layer in range(GHOST):
                    z_first[k, f, layer] = head[pl.ds(layer, 8, stride=8), :]
                    z_last[k, f, layer] = tail[pl.ds(8 - GHOST + layer, 8, stride=8), :]

    for i in range(LINKS):
        pltpu.make_async_copy(items.at[i], own_items.at[i, rows], item_sems.at[i]).wait()
    for copy in whole:
        copy.wait()


def faces(fields, plan, place, links, cells, received, after, carried):
    count, first, last = len(fields), fields[0], fields[0] > 0
    held_chunks = 3 * len(chunks_of(fields))
    z_shape = jax.ShapeDtypeStruct((SLOTS, FIELDS, GHOST, 8, 128), F32)
    scratch = [
        pltpu.VMEM((count,) + PATCH_SHAPE[1:], F32),
        pltpu.VMEM((count,) + TURNED_SHAPE[1:], F32),
        pltpu.VMEM((LINKS, count * GHOST * 8, 128), F32),
        pltpu.SemaphoreType.DMA((count, SLOTS, 2)),
        pltpu.SemaphoreType.DMA((LINKS,)),
        pltpu.SemaphoreType.DMA((count,)),
    ]
    if last:
        scratch = [
            pltpu.VMEM((2, first, SLOTS, 64, 128), F32),
            pltpu.SemaphoreType.DMA((2,)),
        ] + scratch
    inputs = [held(cells)] + list(received) + [after] + [held(x) for x in carried]
    return pl.pallas_call(
        functools.partial(faces_kernel, fields),
        out_shape=[
            pltpu.HBM(PATCH_SHAPE, F32),
            pltpu.HBM((PLANE, 2, ITEM_ROWS, 128), F32),
            pltpu.HBM((LINKS, ITEM_ROWS, 128), F32),
        ]
        + [z_shape] * (2 * last),
        in_specs=[SMEM] * 3 + [HBM] + [ANY] * (held_chunks + 1) + [HBM] * len(carried),
        out_specs=[HBM] * 3 + [VMEM] * (2 * last),
        scratch_shapes=scratch,
        input_output_aliases={held_chunks + 5 + i: i for i in range(len(carried))},
        compiler_params=pltpu.CompilerParams(vmem_limit_bytes=16 * MIB),
        cost_estimate=LONG if last else None,
        name="faces",
    )(plan, place, links, *inputs)


def clamped(x, y):
    return jnp.minimum(jnp.maximum(x, jnp.minimum(y, 0.0)), jnp.maximum(y, 0.0))


def euler_terms(w, normal):
    density, velocity, pressure = w[0], w[1:4], w[4]
    speed = velocity[normal]
    momentum = [density * v for v in velocity]
    kinetic = momentum[0] * velocity[0] + momentum[1] * velocity[1] + momentum[2] * velocity[2]
    energy = 1.5 * pressure + 0.5 * kinetic
    flux = [momentum[normal]]
    for i in range(3):
        term = momentum[i] * speed
        flux.append(term + pressure if i == normal else term)
    flux.append((energy + pressure) * speed)
    stiff = GAMMA * pressure
    signal = jnp.abs(speed) + stiff * lax.rsqrt(stiff * density)
    return [density] + momentum + [energy], flux, signal


def sweep(get, put, normal, first, last):
    w, d, a, b = {}, {}, {}, {}
    prev, left = None, None
    start = first - 2
    for i in range(start, last + 4):
        w[i] = get(i)
        if i == start:
            continue
        d[i - 1] = [hi - lo for hi, lo in zip(w[i], w[i - 1])]
        m = i - 2
        if m <= start:
            continue
        a[m] = [
            clamped(0.5 * mid - (1.0 / 12.0) * (up - down), mid)
            for down, mid, up in zip(d[m - 1], d[m], d[m + 1])
        ]
        b[m + 1] = [mid - part for mid, part in zip(d[m], a[m])]
        if m < first:
            continue
        if m > first:
            lower = [v - clamped(y, 2.0 * x) for v, x, y in zip(w[m], a[m], b[m])]
            right = euler_terms(lower, normal)
            fastest = jnp.maximum(left[2], right[2])
            flux = [
                gl + gr - fastest * (ur - ul)
                for gl, gr, ul, ur in zip(left[1], right[1], left[0], right[0])
            ]
            if prev is not None:
                put(m - 1, [new - old for new, old in zip(flux, prev)])
            elif m > 0:
                put(m - 1, flux)
            prev = flux
        if m <= last:
            upper = [v + clamped(x, 2.0 * y) for v, x, y in zip(w[m], a[m], b[m])]
            left = euler_terms(upper, normal)
    if last + 1 < EDGE:
        put(last + 1, [-v for v in prev])


def inner_kernel(place, links, patches_in, z_below, z_above, out, rim_out, table, *scratch):
    turned, patches, change, partial, rim, sems, out_sems = scratch
    loads = [
        pltpu.make_async_copy(patches_in.at[:, k], patches.at[:, k], sems.at[k])
        for k in range(SLOTS)
    ]
    for load in loads:
        load.start()
    me = place[0]
    for i in range(LINKS):
        entry = links[me * LINKS + i]
        owner = entry // SLOTS
        source = (entry % SLOTS) * 4 + (i % 4 ^ 1)
        rank = jnp.int32(0)
        for j in range(LINKS - 1):
            same = jnp.logical_and(links[owner * LINKS + j] // SLOTS == me, j < source)
            rank = rank + same.astype(jnp.int32)
        table[i] = owner
        table[LINKS + i] = jnp.minimum(rank, 1)
        table[2 * LINKS + i] = source
    for load in loads:
        load.wait()
    for f in range(FIELDS):
        turn(patches, turned, f)

    def z_sweep(k, carry):
        def get(i):
            if i < 0:
                u = [z_below[k, f, i + GHOST] for f in range(FIELDS)]
            elif i >= EDGE:
                u = [z_above[k, f, i - EDGE] for f in range(FIELDS)]
            else:
                rows = pl.ds(i % 8, 8, stride=8)
                u = [patches[f, k, i // 8, rows, :] for f in range(FIELDS)]
            return primitives(u)

        def put(i, values):
            rows = pl.ds(i % 8, 8, stride=8)
            for f in range(FIELDS):
                partial[f, k, i // 8, rows, :] = (
                    patches[f, k, i // 8, rows, :] - (0.5 * DT_DX) * values[f]
                )

        sweep(get, put, 2, -1, EDGE - 1)
        return carry

    lax.fori_loop(0, SLOTS, z_sweep, 0)

    def plane_sweep(direction, g, put):
        def get(i):
            block, rows = turned_rows(direction, i, g)
            w = primitives([turned[f, block, rows, :] for f in range(FIELDS)])
            end, at = (0, i) if i < RIM else (1, i - EDGE + RIM)
            if 0 <= at < RIM:
                for f in range(FIELDS):
                    rim[direction, end, at, f, g] = w[f]
            return w

        sweep(get, put, direction, 2, EDGE - 4)

    def y_sweep(g, carry):
        def put(i, values):
            block, rows = turned_rows(1, i, g)
            for f in range(FIELDS):
                change[f, block, rows, :] = values[f]

        for i in (0, 1, EDGE - 2, EDGE - 1):
            put(i, [jnp.zeros((8, 128), F32)] * FIELDS)
        plane_sweep(1, g, put)
        return carry

    lax.fori_loop(0, 4, y_sweep, 0)

    def x_sweep(g, carry):
        def put(i, values):
            block, rows = turned_rows(0, i, g)
            for f in range(FIELDS):
                change[f, block, rows, :] = change[f, block, rows, :] + values[f]

        plane_sweep(0, g, put)
        return carry

    lax.fori_loop(0, 4, x_sweep, 0)
    rim_copy = pltpu.make_async_copy(rim, rim_out, out_sems.at[FIELDS])
    rim_copy.start()
    copies = []
    for f in range(FIELDS):
        add_turned(change, partial, f, partial.at[f])
        copies.append(pltpu.make_async_copy(partial.at[f], out.at[f], out_sems.at[f]))
        copies[f].start()
    for copy in copies + [rim_copy]:
        copy.wait()


def add_turned(change, partial, f, result):
    back = (0.5 * DT_DX) * jnp.transpose(flat(change, f))
    for k in range(SLOTS):
        for c in range(LAYERS):
            n = (k * LAYERS + c) * 8
            for b in range(8):
                rows = pl.ds(8 * b, 8)
                result[k, c, rows, :] = (
                    partial[f, k, c, rows, :] - back[n : n + 8, 128 * b : 128 * (b + 1)]
                )


def inner(place, links, patches, z_below, z_above):
    return pl.pallas_call(
        inner_kernel,
        out_shape=[
            pltpu.HBM(PATCH_SHAPE, F32),
            pltpu.HBM(RIM_SHAPE, F32),
            jax.ShapeDtypeStruct((3 * LINKS,), jnp.int32),
        ],
        in_specs=[SMEM, SMEM, HBM, VMEM, VMEM],
        out_specs=[HBM, HBM, SMEM],
        scratch_shapes=[
            pltpu.VMEM(TURNED_SHAPE, F32),
            pltpu.VMEM(PATCH_SHAPE, F32),
            pltpu.VMEM(TURNED_SHAPE, F32),
            pltpu.VMEM(PATCH_SHAPE, F32),
            pltpu.VMEM(RIM_SHAPE, F32),
            pltpu.SemaphoreType.DMA((SLOTS,)),
            pltpu.SemaphoreType.DMA((FIELDS + 1,)),
        ],
        compiler_params=pltpu.CompilerParams(vmem_limit_bytes=24 * MIB),
        cost_estimate=LONG,
        name="inner",
    )(place, links, held(patches), z_below, z_above)


def outer_kernel(place, table, rim_in, arrived, own_items, partial_in, out, *scratch):
    rim, items, ghosts, change, partial, result, item_sems, sems, out_sems = scratch
    me = place[0]
    for i in range(LINKS):
        owner, rank, source = table[i], table[LINKS + i], table[2 * LINKS + i]

        @pl.when(owner != me)
        def _(i=i, owner=owner, rank=rank):
            pltpu.make_async_copy(arrived.at[owner, rank], items.at[i], item_sems.at[i]).start()

        @pl.when(owner == me)
        def _(i=i, source=source):
            pltpu.make_async_copy(own_items.at[source], items.at[i], item_sems.at[i]).start()

    loads = [
        pltpu.make_async_copy(rim_in, rim, sems.at[0]),
        pltpu.make_async_copy(partial_in, partial, sems.at[1]),
    ]
    for load in loads:
        load.start()
    change[...] = jnp.zeros(TURNED_SHAPE, F32)
    for i in range(LINKS):
        pltpu.make_async_copy(own_items.at[i], items.at[i], item_sems.at[i]).wait()
    for side in range(4):
        blocks = [items[k * 4 + side] for k in range(SLOTS)]
        for g, block in enumerate(block_transpose(blocks)):
            ghosts[side, g] = block
    loads[0].wait()

    def border(g, carry):
        for direction in (1, 0):

            def get(i):
                if 0 <= i < EDGE:
                    end, at = (0, i) if i < RIM else (1, i - EDGE + RIM)
                    return [rim[direction, end, at, f, g] for f in range(FIELDS)]
                side, layer = (0, i + GHOST) if i < 0 else (1, i - EDGE)
                rows = [pl.ds((f * GHOST + layer) * 8, 8) for f in range(FIELDS)]
                return primitives([ghosts[2 * direction + side, g, at, :] for at in rows])

            def put(i, values):
                block, rows = turned_rows(direction, i, g)
                for f in range(FIELDS):
                    change[f, block, rows, :] = change[f, block, rows, :] + values[f]

            sweep(get, put, direction, -1, 1)
            sweep(get, put, direction, EDGE - 3, EDGE - 1)
        return carry

    lax.fori_loop(0, 4, border, 0)
    loads[1].wait()
    copies = []
    for f in range(FIELDS):
        add_turned(change, partial, f, result.at[f])
        copies.append(pltpu.make_async_copy(result.at[f], out.at[:, f], out_sems.at[f]))
        copies[f].start()
    for copy in copies:
        copy.wait()


def outer(place, table, rim, arrived, own_items, partial):
    return pl.pallas_call(
        outer_kernel,
        out_shape=jax.ShapeDtypeStruct((SLOTS, FIELDS, LAYERS, 64, 128), F32),
        in_specs=[SMEM, SMEM] + [HBM] * 4,
        out_specs=HBM,
        scratch_shapes=[
            pltpu.VMEM(RIM_SHAPE, F32),
            pltpu.VMEM((LINKS, ITEM_ROWS, 128), F32),
            pltpu.VMEM((4, 4, ITEM_ROWS, 128), F32),
            pltpu.VMEM(TURNED_SHAPE, F32),
            pltpu.VMEM(PATCH_SHAPE, F32),
            pltpu.VMEM(PATCH_SHAPE, F32),
            pltpu.SemaphoreType.DMA((LINKS,)),
            pltpu.SemaphoreType.DMA((2,)),
            pltpu.SemaphoreType.DMA((FIELDS,)),
        ],
        compiler_params=pltpu.CompilerParams(vmem_limit_bytes=24 * MIB),
        name="outer",
    )(place, table, held(rim), held(arrived), held(own_items), held(partial))


def local(cells, moves, neighbours):
    tiled = cells.reshape(SLOTS, FIELDS, LAYERS, 8, 8, 128).transpose(0, 1, 2, 4, 3, 5)
    tiled = tiled.reshape(SLOTS, FIELDS * LAYERS, 64, 128)
    plan = moves[lax.axis_index(("gx", "gy", "gz"))].reshape(-1)
    place = lax.axis_index(("gx", "gy")).reshape(1)
    links = neighbours.reshape(-1)

    got, after = migrate(plan, tiled)
    made = ()
    for fields in GROUPS:
        received = [got[r, c] for c in chunks_of(fields) for r in range(3)]
        made = faces(fields, plan, place, links, tiled, received, after, made)
    patches, send, own_items, z_first, z_last = made

    arrived = lax.all_to_all(send, ("gx", "gy"), 0, 0, tiled=True)
    layers = lax.axis_size("gz")
    up = [(i, (i + 1) % layers) for i in range(layers)]
    down = [(j, i) for i, j in up]
    z_below = lax.ppermute(z_last, "gz", up)
    z_above = lax.ppermute(z_first, "gz", down)
    partial, rim, table = inner(place, links, patches, z_below, z_above)
    result = outer(place, table, rim, arrived, own_items, partial)
    result = result.reshape(SLOTS, FIELDS, LAYERS, 8, 8, 128).transpose(0, 1, 2, 4, 3, 5)
    return result.reshape(cells.shape)


def solution(mesh):
    return jax.shard_map(
        local,
        mesh=mesh,
        in_specs=(P(("gx", "gy", "gz"), None, None, None), P(), P()),
        out_specs=P(("gx", "gy", "gz"), None, None, None),
        check_vma=False,
    )
```
